256 devices in a mesh: replica: 2 (over core), fsdp: 128 (over x, y, z).
Axes of the slice: x: 4, y: 4, z: 8, core: 2. Of those that a mesh axis runs over, the one named last changes fastest.
Arguments:
- grad_parts: bfloat16 [2, 512, 16, 8192], P('replica', 'fsdp'), may hold values from -1.5 to 1.5
- left_basis: float32 [256, 512, 512], P(('replica', 'fsdp')), may hold values from -0.25 to 0.25
- right_basis: float32 [256, 512, 512], P(('replica', 'fsdp')), may hold values from -0.25 to 0.25
- first_moment: float32 [256, 512, 512], P(('replica', 'fsdp')), may hold values from -1.5 to 1.5
- second_moment: float32 [256, 512, 512], P(('replica', 'fsdp')), may hold values from 0.001 to 0.1
- left_factor: float32 [256, 512, 512], P(('replica', 'fsdp')), may hold values from -1.5 to 1.5
- right_factor: float32 [256, 512, 512], P(('replica', 'fsdp')), may hold values from -1.5 to 1.5
- owner_table: int32 [2, 128], replicated, may hold values from 0 to 127, each once within a row
Outputs:
- update: float32 [512, 16, 8192], P('fsdp', 'replica')
- new_first: float32 [256, 512, 512], P(('replica', 'fsdp'))
- new_second: float32 [256, 512, 512], P(('replica', 'fsdp'))
- new_left: float32 [256, 512, 512], P(('replica', 'fsdp'))
- new_right: float32 [256, 512, 512], P(('replica', 'fsdp'))
The draws below stay inside these ranges and needn't reach their ends.
Inputs may be any that keep to these rules, and one draw needn't show every extreme that they name: Each row of owner_table names every block of its half once.
All inputs are finite; a program needn't handle non-finite values.
Results may differ from the reference program's by a relative error of at most 0.0003.
Values may be sent and summed in bfloat16 or wider, within the bound.
A program may use at most 64 MiB of HBM per device.

```python
import math
import jax
import jax.numpy as jnp
from jax import lax

B = 512
C = 8192
HALF_ROWS = 8
BLOCK_ROWS = 16
HALF_BLOCKS = 128
SLOTS = 256
N_REPLICA = 2


def shard_levels(stream_key, shape, pieces, low, top_value):
    def one(dim, shards_of):
        draws = jax.random.uniform(jax.random.fold_in(jax.random.fold_in(stream_key, 6), dim), (shards_of,), jnp.float32, low / len(pieces), top_value / len(pieces))
        return jnp.repeat(jnp.exp(draws), shape[dim] // shards_of).reshape((-1,) + (1,) * (len(shape) - dim - 1))

    level = one(*pieces[0])
    for cut in pieces[1:]:
        level = level * one(*cut)
    return level


def scatter_about(key, shape, spread, limit, shards=(), dtype=jnp.bfloat16):
    values = jax.random.normal(key, shape, jnp.float32) * spread
    if len(shards) > 0:
        values = shard_levels(key, shape, shards, -0.22, 0.18) * values
    return jnp.clip(values, min=-limit, max=limit).astype(dtype)


def setup_inputs(seed: int = 0) -> dict:
    keys = jax.random.split(jax.random.key(seed), 9)
    grad_parts = scatter_about(keys[0], (N_REPLICA, B, BLOCK_ROWS, C), 0.1, 1.5, ((0, 2), (1, 128)))
    left_basis = scatter_about(keys[1], (SLOTS, B, B), B ** -0.5, 0.25, ((0, 256),), jnp.float32)
    right_basis = scatter_about(keys[2], (SLOTS, B, B), B ** -0.5, 0.25, ((0, 256),), jnp.float32)
    first_moment = scatter_about(keys[3], (SLOTS, B, B), 0.1, 1.5, ((0, 256),), jnp.float32)
    second_moment = jnp.clip(jnp.exp(math.log(0.1) - 4.6051702 * jax.random.uniform(keys[4], (SLOTS, B, B), jnp.float32) ** shard_levels(keys[4], (SLOTS, B, B), ((0, 256),), -0.2, 0.2)), 0.001, 0.1)
    left_factor = scatter_about(keys[5], (SLOTS, B, B), 0.1, 1.5, ((0, 256),), jnp.float32)
    right_factor = scatter_about(keys[6], (SLOTS, B, B), 0.1, 1.5, ((0, 256),), jnp.float32)
    owner_table = jax.vmap(lambda own: jax.random.permutation(own, HALF_BLOCKS))(jax.random.split(keys[7], N_REPLICA)).reshape((N_REPLICA, HALF_BLOCKS)).astype(jnp.int32)
    return {"grad_parts": grad_parts, "left_basis": left_basis, "right_basis": right_basis, "first_moment": first_moment, "second_moment": second_moment, "left_factor": left_factor, "right_factor": right_factor, "owner_table": owner_table}


def reference(grad_parts, left_basis, right_basis, first_moment, second_moment, left_factor, right_factor, owner_table):
    highest = lax.Precision.HIGHEST
    col_blocks = C // B
    summed = grad_parts[0].astype(jnp.float32) + grad_parts[1].astype(jnp.float32)
    halves = summed.reshape(B, 2, HALF_ROWS, col_blocks, B).transpose(1, 2, 3, 0, 4).reshape(2, HALF_BLOCKS, B, B)
    first_table = owner_table[0].astype(jnp.int32)
    second_table = owner_table[1].astype(jnp.int32)
    blocks = jnp.concatenate([halves[0][first_table], halves[1][second_table]], axis=0)
    left_rot = jnp.einsum('sji,sjk->sik', left_basis, blocks, precision=highest)
    rotated = jnp.einsum('sik,skl->sil', left_rot, right_basis, precision=highest)
    new_first = 0.95 * first_moment + 0.05 * rotated
    new_second = 0.95 * second_moment + 0.05 * rotated * rotated
    scaled = new_first / (jnp.sqrt(new_second) + 1e-08)
    back_left = jnp.einsum('sij,sjk->sik', left_basis, scaled, precision=highest)
    back = jnp.einsum('sik,slk->sil', back_left, right_basis, precision=highest)
    new_left = 0.95 * left_factor + 0.05 * jnp.einsum('sik,sjk->sij', blocks, blocks, precision=highest)
    new_right = 0.95 * right_factor + 0.05 * jnp.einsum('ski,skj->sij', blocks, blocks, precision=highest)
    placed = jnp.zeros((2, HALF_BLOCKS, B, B), jnp.float32)
    placed = placed.at[0, first_table].set(back[:HALF_BLOCKS])
    placed = placed.at[1, second_table].set(back[HALF_BLOCKS:])
    update = placed.reshape(2, HALF_ROWS, col_blocks, B, B).transpose(3, 0, 1, 2, 4).reshape(B, BLOCK_ROWS, C)
    return (update, new_first, new_second, new_left, new_right)
```

```python
import functools

import jax
import jax.numpy as jnp
from jax import lax
from jax.experimental import pallas as pl
from jax.experimental.pallas import tpu as pltpu
from jax.sharding import PartitionSpec as P

MESH = pl.DeviceIdType.MESH
N = 128
B = 512
TINY = 1e-33
F32, BF16, I32 = jnp.float32, jnp.bfloat16, jnp.int32
CHUNKS = 4
WIDE = 8192 // CHUNKS


def offset(me, t):
    u = lax.rem(t, 8)
    dz = jnp.where(lax.rem(u, 2) == 1, (u + 1) // 2, lax.rem(8 - u // 2, 8))
    z = lax.rem(lax.rem(me, 8) + dz, 8)
    y = lax.rem(lax.rem(me // 8, 4) + lax.rem(t // 8, 4), 4)
    x = lax.rem(me // 32 + t // 32, 4)
    return x * 32 + y * 8 + z


def split(x):
    high = x.astype(BF16)
    return high, (x - high.astype(F32)).astype(BF16)


def dot3(a, b, dims=((1,), (0,))):
    one = functools.partial(
        lax.dot_general,
        dimension_numbers=(dims, ((), ())),
        preferred_element_type=F32,
    )
    return one(a[0], b[0]) + (one(a[0], b[1]) + one(a[1], b[0]))


def pack(q):
    return (q[:, :256] << 16) | (q[:, 256:] & 0xFFFF)


def unpack(w):
    return w >> 16, (w << 16) >> 16


def rows(start, size=8):
    return pl.ds(pl.multiple_of(start, 8), size)


def step_kernel(
    g_hbm, l_hbm, r_hbm, m_hbm, v_hbm, lf_hbm, rf_hbm, table,
    back_words, back_scales, new_first, new_second, new_left, new_right,
    g, l, r, m, v, lf, rf,
    own, sib_out, sib_in, pieces, scales, out_words, out_scales, in_words, in_scales,
    blocks, lh, ll, lth, ltl, rh, rl, rth, rtl, bh, bl, wh, wl, ret_words, ret_scales,
    g_sem, in_sem, sib_send, sib_recv, fwd_send, fwd_recv, bwd_send, bwd_recv,
):
    rep = lax.axis_index("replica")
    me = lax.axis_index("fsdp")
    wides = [pl.ds(j * WIDE, WIDE) for j in range(CHUNKS)]
    loads = [
        pltpu.make_async_copy(g_hbm.at[0, :, :, w], g.at[:, :, w], g_sem.at[j])
        for j, w in enumerate(wides)
    ]
    pairs = ((l_hbm, l), (r_hbm, r), (m_hbm, m), (v_hbm, v), (lf_hbm, lf), (rf_hbm, rf))
    others = [
        pltpu.make_async_copy(a.at[0], b, in_sem.at[j]) for j, (a, b) in enumerate(pairs)
    ]
    for copy in loads + others:
        copy.start()

    barrier = pltpu.get_barrier_semaphore()
    pl.semaphore_signal(barrier, inc=1, device_id=(1 - rep, me), device_id_type=MESH)

    def greet(t, c):
        pl.semaphore_signal(
            barrier, inc=1, device_id=(rep, offset(me, t)), device_id_type=MESH
        )
        return c

    lax.fori_loop(1, N, greet, 0)

    for copy in loads:
        copy.wait()

    def part(c, carry):
        cols = pl.ds(pl.multiple_of(c * B, B), B)
        for pair in range(2):
            sent = []
            for i in (2 * pair, 2 * pair + 1):
                x = g[i, :, cols].astype(F32)
                low, high = x[:8], x[8:]
                own[i, :, cols] = jnp.where(rep == 0, low, high)
                sent.append(jnp.where(rep == 0, high, low))
            sib_out[pair, :, cols] = jnp.concatenate(sent, axis=0).astype(BF16)
        return carry

    lax.fori_loop(0, 16, part, 0)
    pl.semaphore_wait(barrier, N)

    exchange = [
        pltpu.make_async_remote_copy(
            src_ref=sib_out.at[:, :, w],
            dst_ref=sib_in.at[:, :, w],
            send_sem=sib_send.at[j],
            recv_sem=sib_recv.at[j],
            device_id=(1 - rep, me),
            device_id_type=MESH,
        )
        for j, w in enumerate(wides)
    ]
    for copy in exchange:
        copy.start()

    def code(c, carry):
        cols = pl.ds(pl.multiple_of(c * B, B), B)
        xs = []
        for pair in range(2):
            y = sib_in[pair, :, cols].astype(F32)
            xs.append(own[2 * pair, :, cols] + y[:8])
            xs.append(own[2 * pair + 1, :, cols] + y[8:])
        top = functools.reduce(jnp.maximum, [jnp.abs(x) for x in xs])
        top = jnp.maximum(jnp.max(top, axis=1, keepdims=True), TINY)
        inverse = 32767.0 / top
        for i, x in enumerate(xs):
            w = pack(jnp.round(x * inverse).astype(I32))
            for half in range(2):
                pieces[pl.ds(c * 8 + i * 2 + half, 8, stride=128), :] = w[
                    :, half * 128 : half * 128 + 128
                ]
        scales[pl.ds(c, 8, stride=16), :] = jnp.broadcast_to(
            top * (1.0 / 32767.0), (8, 128)
        )
        return carry

    for j, copy in enumerate(exchange):
        copy.wait()
        lax.fori_loop(j * (16 // CHUNKS), (j + 1) * (16 // CHUNKS), code, 0)

    def take(q):
        k = table[rep, q]
        return pieces.reshape(N, 8, 128)[k], scales[pl.ds(k, 1), :]

    def send(t, c):
        q = offset(me, t)
        word, scale = take(q)
        out_words[rows(t * 8), :] = word
        out_scales[t] = scale
        pltpu.make_async_remote_copy(
            src_ref=out_words.at[rows(t * 8)],
            dst_ref=in_words.at[rows(me * 8)],
            send_sem=fwd_send.at[0],
            recv_sem=fwd_recv.at[0],
            device_id=(rep, q),
            device_id_type=MESH,
        ).start()
        pltpu.make_async_remote_copy(
            src_ref=out_scales.at[t],
            dst_ref=in_scales.at[me],
            send_sem=fwd_send.at[1],
            recv_sem=fwd_recv.at[1],
            device_id=(rep, q),
            device_id_type=MESH,
        ).start()
        return c

    lax.fori_loop(1, N, send, 0)
    word, scale = take(me)
    in_words[rows(me * 8), :] = word
    in_scales[me] = scale

    for copy in others:
        copy.wait()
    for x, h, w, th, tw in ((l, lh, ll, lth, ltl), (r, rh, rl, rth, rtl)):
        h[...], w[...] = split(x[...])
        th[...], tw[...] = split(x[...].T)

    def arrived(sems, words, lines):
        pltpu.make_async_copy(
            words.at[rows(0, 8 * (N - 1))], words.at[rows(0, 8 * (N - 1))], sems.at[0]
        ).wait()
        pltpu.make_async_copy(
            lines.at[pl.ds(0, N - 1)], lines.at[pl.ds(0, N - 1)], sems.at[1]
        ).wait()

    arrived(fwd_recv, in_words, in_scales)

    upper = lax.broadcasted_iota(I32, (8, 128), 0) < 4

    def decode(j, c):
        scale = jnp.where(
            upper,
            jnp.broadcast_to(in_scales[2 * j], (8, 128)),
            jnp.broadcast_to(in_scales[2 * j + 1], (8, 128)),
        )
        for half in range(2):
            a, b = unpack(in_words[pl.ds(j * 16 + half, 8, stride=2), :])
            for q, col in ((a, half), (b, half + 2)):
                blocks[rows(j * 8), pl.ds(col * 128, 128)] = q.astype(F32) * scale
        return c

    lax.fori_loop(0, 64, decode, 0, unroll=4)

    bh[...], bl[...] = split(blocks[...])
    wh[...], wl[...] = split(dot3((bh[...], bl[...]), (rh[...], rl[...])))
    rotated = dot3((lth[...], ltl[...]), (wh[...], wl[...]))
    new_first[...] = 0.95 * m[...] + 0.05 * rotated
    new_second[...] = 0.95 * v[...] + 0.05 * rotated * rotated
    scaled = new_first[...] / (jnp.sqrt(new_second[...]) + 1e-08)
    wh[...], wl[...] = split(scaled)
    left = split(dot3((lh[...], ll[...]), (wh[...], wl[...])))
    own_back = dot3(left, (rth[...], rtl[...]))
    blocks[...] = own_back

    def encode(j, c):
        x = blocks[rows(j * 8), :]
        top = jnp.max(jnp.max(jnp.abs(x), axis=1, keepdims=True), axis=0, keepdims=True)
        top = jnp.maximum(top, TINY)
        w = pack(jnp.round(x * (32767.0 / top)).astype(I32))
        for half in range(2):
            ret_words[pl.ds(j * 16 + half, 8, stride=2), :] = w[
                :, half * 128 : half * 128 + 128
            ]
        scale = jnp.broadcast_to(top * (1.0 / 32767.0), (1, 128))
        ret_scales[2 * j] = scale
        ret_scales[2 * j + 1] = scale
        return c

    lax.fori_loop(0, 64, encode, 0, unroll=4)

    def give(t, c):
        q = offset(me, t)
        pltpu.make_async_remote_copy(
            src_ref=ret_words.at[rows(q * 8)],
            dst_ref=back_words.at[rows(me * 8)],
            send_sem=bwd_send.at[0],
            recv_sem=bwd_recv.at[0],
            device_id=(rep, q),
            device_id_type=MESH,
        ).start()
        pltpu.make_async_remote_copy(
            src_ref=ret_scales.at[q],
            dst_ref=back_scales.at[me],
            send_sem=bwd_send.at[1],
            recv_sem=bwd_recv.at[1],
            device_id=(rep, q),
            device_id_type=MESH,
        ).start()
        return c

    lax.fori_loop(1, N, give, 0)
    back_words[rows(me * 8), :] = ret_words[rows(me * 8), :]
    back_scales[me] = ret_scales[me]

    pair = (bh[...], bl[...])
    new_left[...] = 0.95 * lf[...] + 0.05 * dot3(pair, pair, ((1,), (1,)))
    new_right[...] = 0.95 * rf[...] + 0.05 * dot3(pair, pair, ((0,), (0,)))

    arrived(fwd_send, out_words, out_scales)
    arrived(bwd_send, ret_words, ret_scales)
    arrived(bwd_recv, back_words, back_scales)


def write_kernel(
    words, lines, first, second, left, right, table,
    update_hbm, first_hbm, second_hbm, left_hbm, right_hbm,
    pieces, scales, update, sems,
):
    rep = lax.axis_index("replica")
    pairs = ((first, first_hbm), (second, second_hbm), (left, left_hbm), (right, right_hbm))
    copies = [
        pltpu.make_async_copy(a, b.at[0], sems.at[j]) for j, (a, b) in enumerate(pairs)
    ]
    for copy in copies:
        copy.start()

    def place(q, c):
        k = table[rep, q]
        pieces[rows(k * 8), :] = words[rows(q * 8), :]
        scales[pl.ds(k, 1), :] = lines[q]
        return c

    lax.fori_loop(0, N, place, 0, unroll=8)

    def decode(c, carry):
        scale = scales[pl.ds(c, 8, stride=16), :]
        for i in range(4):
            for half in range(2):
                w = pieces[pl.ds(c * 8 + i * 2 + half, 8, stride=128), :]
                for q, col in zip(unpack(w), (half, half + 2)):
                    cols = pl.ds(pl.multiple_of(c * B + col * 128, 128), 128)
                    update[i, :, cols] = q.astype(F32) * scale
        return carry

    lax.fori_loop(0, 16, decode, 0)
    last = pltpu.make_async_copy(update, update_hbm, sems.at[4])
    last.start()
    for copy in copies + [last]:
        copy.wait()


def body(grad_parts, left_basis, right_basis, first, second, left, right, table):
    hbm = pl.BlockSpec(memory_space=pltpu.HBM)
    vmem = pl.BlockSpec(memory_space=pltpu.VMEM)
    smem = pl.BlockSpec(memory_space=pltpu.SMEM)
    square = jax.ShapeDtypeStruct((B, B), F32)
    halves = [pltpu.VMEM((B, B), BF16)] * 12
    words, lines = pltpu.VMEM((N * 8, 128), I32), pltpu.VMEM((N, 1, 128), F32)
    dma = pltpu.SemaphoreType.DMA
    mids = pl.pallas_call(
        step_kernel,
        out_shape=(
            jax.ShapeDtypeStruct((N * 8, 128), I32),
            jax.ShapeDtypeStruct((N, 1, 128), F32),
            square, square, square, square,
        ),
        in_specs=[hbm] * 7 + [smem],
        out_specs=(vmem,) * 6,
        scratch_shapes=[
            pltpu.VMEM((4, 16, 8192), BF16),
            *[pltpu.VMEM((B, B), F32)] * 6,
            pltpu.VMEM((4, 8, 8192), F32),
            pltpu.VMEM((2, 16, 8192), BF16),
            pltpu.VMEM((2, 16, 8192), BF16),
            words, pltpu.VMEM((N, 128), F32), words, lines, words, lines,
            pltpu.VMEM((B, B), F32),
            *halves,
            words, lines,
            dma((CHUNKS,)), dma((6,)), dma((CHUNKS,)), dma((CHUNKS,)),
            dma((2,)), dma((2,)), dma((2,)), dma((2,)),
        ],
        compiler_params=pltpu.CompilerParams(
            collective_id=0, has_side_effects=True, vmem_limit_bytes=49 * 2**20
        ),
    )(grad_parts, left_basis, right_basis, first, second, left, right, table)
    whole = jax.ShapeDtypeStruct((1, B, B), F32)
    return pl.pallas_call(
        write_kernel,
        out_shape=(
            jax.ShapeDtypeStruct((4, 8, 8192), F32), whole, whole, whole, whole
        ),
        in_specs=[vmem] * 6 + [smem],
        out_specs=(hbm,) * 5,
        scratch_shapes=[
            words, pltpu.VMEM((N, 128), F32), pltpu.VMEM((4, 8, 8192), F32), dma((5,))
        ],
        compiler_params=pltpu.CompilerParams(vmem_limit_bytes=16 * 2**20),
    )(*mids, table)


def solution(mesh):
    owned = P(("replica", "fsdp"), None, None)
    return jax.shard_map(
        body,
        mesh=mesh,
        in_specs=(P("replica", "fsdp", None, None),) + (owned,) * 6 + (P(),),
        out_specs=(P("fsdp", "replica", None),) + (owned,) * 4,
        check_vma=False,
    )
```

```python
import functools

import jax
import jax.numpy as jnp
from jax import lax
from jax.experimental import pallas as pl
from jax.experimental.pallas import tpu as pltpu
from jax.sharding import PartitionSpec as P

MESH = pl.DeviceIdType.MESH
N = 128
B = 512
TINY = 1e-33
F32, BF16, I32 = jnp.float32, jnp.bfloat16, jnp.int32
CHUNKS = 4
WIDE = 8192 // CHUNKS


def offset(me, t):
    u = lax.rem(t, 8)
    dz = jnp.where(lax.rem(u, 2) == 1, (u + 1) // 2, lax.rem(8 - u // 2, 8))
    z = lax.rem(lax.rem(me, 8) + dz, 8)
    y = lax.rem(lax.rem(me // 8, 4) + lax.rem(t // 8, 4), 4)
    x = lax.rem(me // 32 + t // 32, 4)
    return x * 32 + y * 8 + z


def split(x):
    high = x.astype(BF16)
    return high, (x - high.astype(F32)).astype(BF16)


def dot3(a, b, dims=((1,), (0,))):
    one = functools.partial(
        lax.dot_general,
        dimension_numbers=(dims, ((), ())),
        preferred_element_type=F32,
    )
    return one(a[0], b[0]) + (one(a[0], b[1]) + one(a[1], b[0]))


def pack(q):
    return (q[:, :256] << 16) | (q[:, 256:] & 0xFFFF)


def unpack(w):
    return w >> 16, (w << 16) >> 16


def rows(start, size=8):
    return pl.ds(pl.multiple_of(start, 8), size)


def step_kernel(
    g_hbm, l_hbm, r_hbm, m_hbm, v_hbm, lf_hbm, rf_hbm, table_hbm,
    back_words, back_scales, new_first, new_second, new_left, new_right,
    g, l, r, m, v, lf, rf, table,
    own, sib_out, sib_in, pieces, scales, out_words, out_scales, in_words, in_scales,
    blocks, lh, ll, lth, ltl, rh, rl, rth, rtl, bh, bl, wh, wl, ret_words, ret_scales,
    g_sem, in_sem, sib_send, sib_recv, fwd_send, fwd_recv, bwd_send, bwd_recv,
):
    rep = lax.axis_index("replica")
    me = lax.axis_index("fsdp")
    wides = [pl.ds(j * WIDE, WIDE) for j in range(CHUNKS)]
    loads = [
        pltpu.make_async_copy(g_hbm.at[0, :, :, w], g.at[:, :, w], g_sem.at[j])
        for j, w in enumerate(wides)
    ]
    pairs = (
        (table_hbm, table), (l_hbm.at[0], l), (r_hbm.at[0], r), (m_hbm.at[0], m),
        (v_hbm.at[0], v), (lf_hbm.at[0], lf), (rf_hbm.at[0], rf),
    )
    others = [
        pltpu.make_async_copy(a, b, in_sem.at[j]) for j, (a, b) in enumerate(pairs)
    ]
    for copy in loads:
        copy.start()

    barrier = pltpu.get_barrier_semaphore()
    pl.semaphore_signal(barrier, inc=1, device_id=(1 - rep, me), device_id_type=MESH)

    def greet(t, c):
        pl.semaphore_signal(
            barrier, inc=1, device_id=(rep, offset(me, t)), device_id_type=MESH
        )
        return c

    lax.fori_loop(1, N, greet, 0, unroll=7)
    for copy in others:
        copy.start()

    def part(c):
        cols = pl.ds(c * B, B)
        for pair in range(2):
            sent = []
            for i in (2 * pair, 2 * pair + 1):
                x = g[i, :, cols].astype(F32)
                low, high = x[:8], x[8:]
                own[i, :, cols] = jnp.where(rep == 0, low, high)
                sent.append(jnp.where(rep == 0, high, low))
            sib_out[pair, :, cols] = jnp.concatenate(sent, axis=0).astype(BF16)

    for j, copy in enumerate(loads):
        copy.wait()
        for c in range(j * 16 // CHUNKS, (j + 1) * 16 // CHUNKS):
            part(c)
    pl.semaphore_wait(barrier, N)

    exchange = [
        pltpu.make_async_remote_copy(
            src_ref=sib_out.at[:, :, w],
            dst_ref=sib_in.at[:, :, w],
            send_sem=sib_send.at[j],
            recv_sem=sib_recv.at[j],
            device_id=(1 - rep, me),
            device_id_type=MESH,
        )
        for j, w in enumerate(wides)
    ]
    for copy in exchange:
        copy.start()

    def code(c):
        cols = pl.ds(c * B, B)
        xs = []
        for pair in range(2):
            y = sib_in[pair, :, cols].astype(F32)
            xs.append(own[2 * pair, :, cols] + y[:8])
            xs.append(own[2 * pair + 1, :, cols] + y[8:])
        top = functools.reduce(jnp.maximum, [jnp.abs(x) for x in xs])
        top = jnp.maximum(jnp.max(top, axis=1, keepdims=True), TINY)
        inverse = 32767.0 / top
        for i, x in enumerate(xs):
            w = pack(jnp.round(x * inverse).astype(I32))
            for half in range(2):
                pieces[pl.ds(c * 8 + i * 2 + half, 8, stride=128), :] = w[
                    :, half * 128 : half * 128 + 128
                ]
        scales[pl.ds(c, 8, stride=16), :] = jnp.broadcast_to(
            top * (1.0 / 32767.0), (8, 128)
        )

    for j, copy in enumerate(exchange):
        copy.wait()
        for c in range(j * 16 // CHUNKS, (j + 1) * 16 // CHUNKS):
            code(c)

    def take(q):
        k = table[rep, q]
        return pieces.reshape(N, 8, 128)[k], scales[pl.ds(k, 1), :]

    def gather(t, c):
        word, scale = take(offset(me, t))
        out_words[rows(t * 8), :] = word
        out_scales[t] = scale
        return c

    def sends(words, lines, to_words, to_lines, send_sem, recv_sem, plane, by_step):
        def one(t, c):
            q = offset(me, t)
            slot = t if by_step else q
            pltpu.make_async_remote_copy(
                src_ref=words.at[rows(slot * 8)],
                dst_ref=to_words.at[rows(me * 8)],
                send_sem=send_sem.at[0],
                recv_sem=recv_sem.at[0],
                device_id=(rep, q),
                device_id_type=MESH,
            ).start()
            pltpu.make_async_remote_copy(
                src_ref=lines.at[slot],
                dst_ref=to_lines.at[me],
                send_sem=send_sem.at[1],
                recv_sem=recv_sem.at[1],
                device_id=(rep, q),
                device_id_type=MESH,
            ).start()
            return c

        lax.fori_loop(max(1, plane * 32), plane * 32 + 32, one, 0)

    others[0].wait()
    for plane in range(4):
        lax.fori_loop(plane * 32, plane * 32 + 32, gather, 0, unroll=8)
        sends(
            out_words, out_scales, in_words, in_scales,
            fwd_send, fwd_recv.at[plane], plane, True,
        )
    in_words[rows(me * 8), :] = out_words[0:8, :]
    in_scales[me] = out_scales[0]

    def away(plane):
        return lax.rem(me // 32 + 4 - plane, 4)

    for copy in others[1:]:
        copy.wait()
    for x, h, w in ((l, lh, ll), (r, rh, rl)):
        h[...], w[...] = split(x[...])
    rth[...], rtl[...] = split(r[...].T)
    for plane in range(4):
        cols = slice(plane * 128, plane * 128 + 128)
        x = l[rows(away(plane) * 128, 128), :].T
        lth[:, cols], ltl[:, cols] = split(x)

    def arrived(sems, words, lines, count):
        pltpu.make_async_copy(
            words.at[rows(0, 8 * count)], words.at[rows(0, 8 * count)], sems.at[0]
        ).wait()
        pltpu.make_async_copy(
            lines.at[pl.ds(0, count)], lines.at[pl.ds(0, count)], sems.at[1]
        ).wait()

    upper = lax.broadcasted_iota(I32, (8, 128), 0) < 4

    def decode(j):
        scale = jnp.where(
            upper,
            jnp.broadcast_to(in_scales[2 * j], (8, 128)),
            jnp.broadcast_to(in_scales[2 * j + 1], (8, 128)),
        )
        for half in range(2):
            a, b = unpack(in_words[pl.ds(j * 16 + half, 8, stride=2), :])
            for q, col in ((a, half), (b, half + 2)):
                blocks[rows(j * 8), col * 128 : col * 128 + 128] = q.astype(F32) * scale

    for plane in range(4):
        arrived(fwd_recv.at[plane], in_words, in_scales, 31 if plane == 0 else 32)
        first = away(plane) * 16
        for j in range(16):
            decode(first + j)
        some, here = rows(first * 8, 128), slice(plane * 128, plane * 128 + 128)
        high, low = split(blocks[some, :])
        bh[some, :], bl[some, :] = high, low
        wh[here, :], wl[here, :] = split(dot3((high, low), (rh[...], rl[...])))
        if plane == 2:
            new_first[...] = dot3(
                (lth[:, :384], ltl[:, :384]), (wh[:384, :], wl[:384, :])
            )
    rotated = new_first[...] + dot3(
        (lth[:, 384:], ltl[:, 384:]), (wh[384:, :], wl[384:, :])
    )
    first = 0.95 * m[...] + 0.05 * rotated
    second = 0.95 * v[...] + 0.05 * rotated * rotated
    new_first[...] = first
    new_second[...] = second
    wh[...], wl[...] = split(first / (jnp.sqrt(second) + 1e-08))

    def encode(j, x):
        top = jnp.max(jnp.max(jnp.abs(x), axis=0, keepdims=True), axis=1, keepdims=True)
        top = jnp.maximum(top, TINY)
        w = pack(jnp.round(x * (32767.0 / top)).astype(I32))
        for half in range(2):
            ret_words[pl.ds(j * 16 + half, 8, stride=2), :] = w[
                :, half * 128 : half * 128 + 128
            ]
        scale = jnp.broadcast_to(top * (1.0 / 32767.0), (1, 128))
        ret_scales[2 * j] = scale
        ret_scales[2 * j + 1] = scale

    for plane in range(4):
        first = lax.rem(me // 32 + plane, 4) * 16
        some = rows(first * 8, 128)
        part_left = split(dot3((lh[some, :], ll[some, :]), (wh[...], wl[...])))
        back = dot3(part_left, (rth[...], rtl[...]))
        for j in range(16):
            encode(first + j, back[j * 8 : j * 8 + 8, :])
        sends(
            ret_words, ret_scales, back_words, back_scales,
            bwd_send, bwd_recv, plane, False,
        )
    back_words[rows(me * 8), :] = ret_words[rows(me * 8), :]
    back_scales[me] = ret_scales[me]

    pair = (bh[...], bl[...])
    new_left[...] = 0.95 * lf[...] + 0.05 * dot3(pair, pair, ((1,), (1,)))
    new_right[...] = 0.95 * rf[...] + 0.05 * dot3(pair, pair, ((0,), (0,)))

    arrived(fwd_send, out_words, out_scales, N - 1)
    arrived(bwd_send, ret_words, ret_scales, N - 1)
    arrived(bwd_recv, back_words, back_scales, N - 1)


def write_kernel(
    words, lines, first, second, left, right, table_hbm,
    update_hbm, first_hbm, second_hbm, left_hbm, right_hbm,
    pieces, scales, update, table, sems,
):
    rep = lax.axis_index("replica")
    fetch = pltpu.make_async_copy(table_hbm, table, sems.at[8])
    fetch.start()
    pairs = ((first, first_hbm), (second, second_hbm), (left, left_hbm), (right, right_hbm))
    copies = [
        pltpu.make_async_copy(a, b.at[0], sems.at[j]) for j, (a, b) in enumerate(pairs)
    ]
    for copy in copies:
        copy.start()
    fetch.wait()

    def place(q, c):
        k = table[rep, q]
        pieces[rows(k * 8), :] = words[rows(q * 8), :]
        scales[pl.ds(k, 1), :] = lines[q]
        return c

    lax.fori_loop(0, N, place, 0, unroll=8)

    def decode(c):
        scale = scales[pl.ds(c, 8, stride=16), :]
        for i in range(4):
            for half in range(2):
                w = pieces[pl.ds(c * 8 + i * 2 + half, 8, stride=128), :]
                for q, col in zip(unpack(w), (half, half + 2)):
                    cols = pl.ds(c * B + col * 128, 128)
                    update[i, :, cols] = q.astype(F32) * scale

    for j in range(CHUNKS):
        for c in range(j * 16 // CHUNKS, (j + 1) * 16 // CHUNKS):
            decode(c)
        w = pl.ds(j * WIDE, WIDE)
        copies.append(
            pltpu.make_async_copy(
                update.at[:, :, w], update_hbm.at[:, :, w], sems.at[4 + j]
            )
        )
        copies[-1].start()
    for copy in copies:
        copy.wait()


def body(grad_parts, left_basis, right_basis, first, second, left, right, table):
    hbm = pl.BlockSpec(memory_space=pltpu.HBM)
    vmem = pl.BlockSpec(memory_space=pltpu.VMEM)
    table_smem = pltpu.SMEM((2, N), I32)
    square = jax.ShapeDtypeStruct((B, B), F32)
    halves = [pltpu.VMEM((B, B), BF16)] * 12
    words, lines = pltpu.VMEM((N * 8, 128), I32), pltpu.VMEM((N, 1, 128), F32)
    dma = pltpu.SemaphoreType.DMA
    mids = pl.pallas_call(
        step_kernel,
        out_shape=(
            jax.ShapeDtypeStruct((N * 8, 128), I32),
            jax.ShapeDtypeStruct((N, 1, 128), F32),
            square, square, square, square,
        ),
        in_specs=[hbm] * 8,
        out_specs=(vmem,) * 6,
        scratch_shapes=[
            pltpu.VMEM((4, 16, 8192), BF16),
            *[pltpu.VMEM((B, B), F32)] * 6,
            table_smem,
            pltpu.VMEM((4, 8, 8192), F32),
            pltpu.VMEM((2, 16, 8192), BF16),
            pltpu.VMEM((2, 16, 8192), BF16),
            words, pltpu.VMEM((N, 128), F32), words, lines, words, lines,
            pltpu.VMEM((B, B), F32),
            *halves,
            words, lines,
            dma((CHUNKS,)), dma((7,)), dma((CHUNKS,)), dma((CHUNKS,)),
            dma((2,)), dma((4, 2)), dma((2,)), dma((2,)),
        ],
        compiler_params=pltpu.CompilerParams(
            collective_id=0, has_side_effects=True, vmem_limit_bytes=49 * 2**20
        ),
    )(grad_parts, left_basis, right_basis, first, second, left, right, table)
    whole = jax.ShapeDtypeStruct((1, B, B), F32)
    return pl.pallas_call(
        write_kernel,
        out_shape=(
            jax.ShapeDtypeStruct((4, 8, 8192), F32), whole, whole, whole, whole
        ),
        in_specs=[vmem] * 6 + [hbm],
        out_specs=(hbm,) * 5,
        scratch_shapes=[
            words, pltpu.VMEM((N, 128), F32), pltpu.VMEM((4, 8, 8192), F32),
            table_smem, dma((9,)),
        ],
        compiler_params=pltpu.CompilerParams(vmem_limit_bytes=16 * 2**20),
    )(*mids, table)


def solution(mesh):
    owned = P(("replica", "fsdp"), None, None)
    return jax.shard_map(
        body,
        mesh=mesh,
        in_specs=(P("replica", "fsdp", None, None),) + (owned,) * 6 + (P(),),
        out_specs=(P("fsdp", "replica", None),) + (owned,) * 4,
        check_vma=False,
    )
```

```python
import functools

import jax
import jax.numpy as jnp
from jax import lax
from jax.experimental import pallas as pl
from jax.experimental.pallas import tpu as pltpu
from jax.sharding import PartitionSpec as P

MESH = pl.DeviceIdType.MESH
N = 128
B = 512
TINY = 1e-33
F32, BF16, I32 = jnp.float32, jnp.bfloat16, jnp.int32
CHUNKS = 4
WIDE = 8192 // CHUNKS


def far_x(plane):
    return jnp.where(plane == 0, 2, jnp.where(plane == 3, 0, 2 * plane - 1))


def turned(step, size, rep):
    return lax.rem(jnp.where(rep == 0, step, size - step), size)


def offset(me, rep, t):
    u = lax.rem(t, 8)
    dz = jnp.where(lax.rem(u, 2) == 0, 4 + u // 2, 4 - (u + 1) // 2)
    dz = jnp.where(u == 7, 0, dz)
    dy, dx = far_x(lax.rem(t // 8, 4)), far_x(t // 32)
    z = lax.rem(lax.rem(me, 8) + turned(dz, 8, rep), 8)
    y = lax.rem(lax.rem(me // 8, 4) + turned(dy, 4, rep), 4)
    x = lax.rem(me // 32 + turned(dx, 4, rep), 4)
    return x * 32 + y * 8 + z


def split(x):
    high = x.astype(BF16)
    return high, (x - high.astype(F32)).astype(BF16)


def dot3(a, b, dims=((1,), (0,))):
    one = functools.partial(
        lax.dot_general,
        dimension_numbers=(dims, ((), ())),
        preferred_element_type=F32,
    )
    return one(a[0], b[0]) + (one(a[0], b[1]) + one(a[1], b[0]))


def pack(q):
    return (q[:, :256] << 16) | (q[:, 256:] & 0xFFFF)


def unpack(w):
    return w >> 16, (w << 16) >> 16


def rows(start, size=8):
    return pl.ds(pl.multiple_of(start, 8), size)


def step_kernel(
    g_hbm, l_hbm, r_hbm, m_hbm, v_hbm, lf_hbm, rf_hbm, table_hbm,
    back_words, back_scales, new_first, new_second, new_left, new_right,
    g, l, r, m, v, lf, rf, table,
    own, sib_out, sib_in, pieces, scales, out_words, out_scales, in_words, in_scales,
    blocks, lh, ll, lth, ltl, rh, rl, rth, rtl, bh, bl, wh, wl, ret_words, ret_scales,
    met, g_sem, in_sem, sib_send, sib_recv, fwd_send, fwd_recv, bwd_send, bwd_recv,
):
    rep = lax.axis_index("replica")
    me = lax.axis_index("fsdp")
    wides = [pl.ds(j * WIDE, WIDE) for j in range(CHUNKS)]
    loads = [
        pltpu.make_async_copy(g_hbm.at[0, :, :, w], g.at[:, :, w], g_sem.at[j])
        for j, w in enumerate(wides)
    ]
    pairs = (
        (table_hbm, table), (l_hbm.at[0], l), (r_hbm.at[0], r), (m_hbm.at[0], m),
        (v_hbm.at[0], v), (lf_hbm.at[0], lf), (rf_hbm.at[0], rf),
    )
    others = [
        pltpu.make_async_copy(a, b, in_sem.at[j]) for j, (a, b) in enumerate(pairs)
    ]
    for copy in loads:
        copy.start()

    x, y, z = me // 32, lax.rem(me // 8, 4), lax.rem(me, 8)
    line = [x * 32 + y * 8 + lax.rem(z + d, 8) for d in range(1, 8)]
    slab = [
        lax.rem(x + d // 4, 4) * 32 + lax.rem(y + d, 4) * 8 + z for d in range(1, 16)
    ]
    barrier = pltpu.get_barrier_semaphore()
    for peer in [(1 - rep, me)] + [(rep, q) for q in line + slab]:
        pl.semaphore_signal(barrier, inc=1, device_id=peer, device_id_type=MESH)
    for copy in others:
        copy.start()

    def part(c):
        cols = pl.ds(c * B, B)
        for pair in range(2):
            sent = []
            for i in (2 * pair, 2 * pair + 1):
                x = g[i, :, cols].astype(F32)
                low, high = x[:8], x[8:]
                own[i, :, cols] = jnp.where(rep == 0, low, high)
                sent.append(jnp.where(rep == 0, high, low))
            sib_out[pair, :, cols] = jnp.concatenate(sent, axis=0).astype(BF16)

    for j, copy in enumerate(loads):
        copy.wait()
        for c in range(j * 16 // CHUNKS, (j + 1) * 16 // CHUNKS):
            part(c)
    pl.semaphore_wait(barrier, 23)

    exchange = [
        pltpu.make_async_remote_copy(
            src_ref=sib_out.at[:, :, w],
            dst_ref=sib_in.at[:, :, w],
            send_sem=sib_send.at[j],
            recv_sem=sib_recv.at[j],
            device_id=(1 - rep, me),
            device_id_type=MESH,
        )
        for j, w in enumerate(wides)
    ]
    for copy in exchange:
        copy.start()
    for q in line:
        pl.semaphore_signal(met, inc=1, device_id=(rep, q), device_id_type=MESH)

    def code(c):
        cols = pl.ds(c * B, B)
        xs = []
        for pair in range(2):
            y = sib_in[pair, :, cols].astype(F32)
            xs.append(own[2 * pair, :, cols] + y[:8])
            xs.append(own[2 * pair + 1, :, cols] + y[8:])
        top = functools.reduce(jnp.maximum, [jnp.abs(x) for x in xs])
        top = jnp.maximum(jnp.max(top, axis=1, keepdims=True), TINY)
        inverse = 32767.0 / top
        for i, x in enumerate(xs):
            w = pack(jnp.round(x * inverse).astype(I32))
            for half in range(2):
                pieces[pl.ds(c * 8 + i * 2 + half, 8, stride=128), :] = w[
                    :, half * 128 : half * 128 + 128
                ]
        scales[pl.ds(c, 8, stride=16), :] = jnp.broadcast_to(
            top * (1.0 / 32767.0), (8, 128)
        )

    for j, copy in enumerate(exchange):
        copy.wait()
        for c in range(j * 16 // CHUNKS, (j + 1) * 16 // CHUNKS):
            code(c)

    def take(q):
        k = table[rep, q]
        return pieces.reshape(N, 8, 128)[k], scales[pl.ds(k, 1), :]

    def gather(t, c):
        word, scale = take(offset(me, rep, t))
        out_words[rows(t * 8), :] = word
        out_scales[t] = scale
        return c

    def sends(words, lines, to_words, to_lines, send_sem, recv_sem, plane, by_step):
        def one(t, c):
            q = offset(me, rep, t)
            slot = t if by_step else q
            pltpu.make_async_remote_copy(
                src_ref=words.at[rows(slot * 8)],
                dst_ref=to_words.at[rows(me * 8)],
                send_sem=send_sem.at[0],
                recv_sem=recv_sem.at[0],
                device_id=(rep, q),
                device_id_type=MESH,
            ).start()
            pltpu.make_async_remote_copy(
                src_ref=lines.at[slot],
                dst_ref=to_lines.at[me],
                send_sem=send_sem.at[1],
                recv_sem=recv_sem.at[1],
                device_id=(rep, q),
                device_id_type=MESH,
            ).start()
            return c

        lax.fori_loop(plane * 32, min(plane * 32 + 32, N - 1), one, 0)

    others[0].wait()
    pl.semaphore_wait(met, 7)
    for plane in range(4):
        lax.fori_loop(plane * 32, plane * 32 + 32, gather, 0, unroll=8)
        sends(
            out_words, out_scales, in_words, in_scales,
            fwd_send, fwd_recv.at[plane], plane, True,
        )
    in_words[rows(me * 8), :] = out_words[rows(8 * (N - 1)), :]
    in_scales[me] = out_scales[N - 1]

    def away(plane):
        return lax.rem(x + 4 - turned(far_x(plane), 4, rep), 4)

    for copy in others[1:]:
        copy.wait()
    for full, h, w in ((l, lh, ll), (r, rh, rl)):
        h[...], w[...] = split(full[...])
    rth[...], rtl[...] = split(r[...].T)
    for plane in range(4):
        cols = slice(plane * 128, plane * 128 + 128)
        lth[:, cols], ltl[:, cols] = split(l[rows(away(plane) * 128, 128), :].T)

    def arrived(sems, words, lines, count):
        pltpu.make_async_copy(
            words.at[rows(0, 8 * count)], words.at[rows(0, 8 * count)], sems.at[0]
        ).wait()
        pltpu.make_async_copy(
            lines.at[pl.ds(0, count)], lines.at[pl.ds(0, count)], sems.at[1]
        ).wait()

    upper = lax.broadcasted_iota(I32, (8, 128), 0) < 4

    def decode(j):
        scale = jnp.where(
            upper,
            jnp.broadcast_to(in_scales[2 * j], (8, 128)),
            jnp.broadcast_to(in_scales[2 * j + 1], (8, 128)),
        )
        for half in range(2):
            a, b = unpack(in_words[pl.ds(j * 16 + half, 8, stride=2), :])
            for q, col in ((a, half), (b, half + 2)):
                blocks[rows(j * 8), col * 128 : col * 128 + 128] = q.astype(F32) * scale

    for plane in range(4):
        arrived(fwd_recv.at[plane], in_words, in_scales, 31 if plane == 3 else 32)
        first = away(plane) * 16
        for j in range(16):
            decode(first + j)
        some, here = rows(first * 8, 128), slice(plane * 128, plane * 128 + 128)
        high, low = split(blocks[some, :])
        bh[some, :], bl[some, :] = high, low
        wh[here, :], wl[here, :] = split(dot3((high, low), (rh[...], rl[...])))
        if plane == 2:
            new_first[...] = dot3(
                (lth[:, :384], ltl[:, :384]), (wh[:384, :], wl[:384, :])
            )
    rotated = new_first[...] + dot3(
        (lth[:, 384:], ltl[:, 384:]), (wh[384:, :], wl[384:, :])
    )
    first = 0.95 * m[...] + 0.05 * rotated
    second = 0.95 * v[...] + 0.05 * rotated * rotated
    new_first[...] = first
    new_second[...] = second
    wh[...], wl[...] = split(first / (jnp.sqrt(second) + 1e-08))

    def encode(j, x):
        top = jnp.max(jnp.max(jnp.abs(x), axis=0, keepdims=True), axis=1, keepdims=True)
        top = jnp.maximum(top, TINY)
        w = pack(jnp.round(x * (32767.0 / top)).astype(I32))
        for half in range(2):
            ret_words[pl.ds(j * 16 + half, 8, stride=2), :] = w[
                :, half * 128 : half * 128 + 128
            ]
        scale = jnp.broadcast_to(top * (1.0 / 32767.0), (1, 128))
        ret_scales[2 * j] = scale
        ret_scales[2 * j + 1] = scale

    for plane in range(4):
        first = lax.rem(x + turned(far_x(plane), 4, rep), 4) * 16
        some = rows(first * 8, 128)
        part_left = split(dot3((lh[some, :], ll[some, :]), (wh[...], wl[...])))
        back = dot3(part_left, (rth[...], rtl[...]))
        for j in range(16):
            encode(first + j, back[j * 8 : j * 8 + 8, :])
        sends(
            ret_words, ret_scales, back_words, back_scales,
            bwd_send, bwd_recv, plane, False,
        )
    back_words[rows(me * 8), :] = ret_words[rows(me * 8), :]
    back_scales[me] = ret_scales[me]

    pair = (bh[...], bl[...])
    new_left[...] = 0.95 * lf[...] + 0.05 * dot3(pair, pair, ((1,), (1,)))
    new_right[...] = 0.95 * rf[...] + 0.05 * dot3(pair, pair, ((0,), (0,)))

    arrived(fwd_send, out_words, out_scales, N - 1)
    arrived(bwd_send, ret_words, ret_scales, N - 1)
    arrived(bwd_recv, back_words, back_scales, N - 1)


def write_kernel(
    words, lines, first, second, left, right, table_hbm,
    update_hbm, first_hbm, second_hbm, left_hbm, right_hbm,
    pieces, scales, update, table, sems,
):
    rep = lax.axis_index("replica")
    fetch = pltpu.make_async_copy(table_hbm, table, sems.at[8])
    fetch.start()
    pairs = ((first, first_hbm), (second, second_hbm), (left, left_hbm), (right, right_hbm))
    copies = [
        pltpu.make_async_copy(a, b.at[0], sems.at[j]) for j, (a, b) in enumerate(pairs)
    ]
    for copy in copies:
        copy.start()
    fetch.wait()

    def place(q, c):
        k = table[rep, q]
        pieces[rows(k * 8), :] = words[rows(q * 8), :]
        scales[pl.ds(k, 1), :] = lines[q]
        return c

    lax.fori_loop(0, N, place, 0, unroll=8)

    def decode(c):
        scale = scales[pl.ds(c, 8, stride=16), :]
        for i in range(4):
            for half in range(2):
                w = pieces[pl.ds(c * 8 + i * 2 + half, 8, stride=128), :]
                for q, col in zip(unpack(w), (half, half + 2)):
                    cols = pl.ds(c * B + col * 128, 128)
                    update[i, :, cols] = q.astype(F32) * scale

    for j in range(CHUNKS):
        for c in range(j * 16 // CHUNKS, (j + 1) * 16 // CHUNKS):
            decode(c)
        w = pl.ds(j * WIDE, WIDE)
        copies.append(
            pltpu.make_async_copy(
                update.at[:, :, w], update_hbm.at[:, :, w], sems.at[4 + j]
            )
        )
        copies[-1].start()
    for copy in copies:
        copy.wait()


def body(grad_parts, left_basis, right_basis, first, second, left, right, table):
    hbm = pl.BlockSpec(memory_space=pltpu.HBM)
    vmem = pl.BlockSpec(memory_space=pltpu.VMEM)
    table_smem = pltpu.SMEM((2, N), I32)
    square = jax.ShapeDtypeStruct((B, B), F32)
    halves = [pltpu.VMEM((B, B), BF16)] * 12
    words, lines = pltpu.VMEM((N * 8, 128), I32), pltpu.VMEM((N, 1, 128), F32)
    dma = pltpu.SemaphoreType.DMA
    mids = pl.pallas_call(
        step_kernel,
        out_shape=(
            jax.ShapeDtypeStruct((N * 8, 128), I32),
            jax.ShapeDtypeStruct((N, 1, 128), F32),
            square, square, square, square,
        ),
        in_specs=[hbm] * 8,
        out_specs=(vmem,) * 6,
        scratch_shapes=[
            pltpu.VMEM((4, 16, 8192), BF16),
            *[pltpu.VMEM((B, B), F32)] * 6,
            table_smem,
            pltpu.VMEM((4, 8, 8192), F32),
            pltpu.VMEM((2, 16, 8192), BF16),
            pltpu.VMEM((2, 16, 8192), BF16),
            words, pltpu.VMEM((N, 128), F32), words, lines, words, lines,
            pltpu.VMEM((B, B), F32),
            *halves,
            words, lines,
            pltpu.SemaphoreType.REGULAR,
            dma((CHUNKS,)), dma((7,)), dma((CHUNKS,)), dma((CHUNKS,)),
            dma((2,)), dma((4, 2)), dma((2,)), dma((2,)),
        ],
        compiler_params=pltpu.CompilerParams(
            collective_id=0, has_side_effects=True, vmem_limit_bytes=49 * 2**20
        ),
    )(grad_parts, left_basis, right_basis, first, second, left, right, table)
    whole = jax.ShapeDtypeStruct((1, B, B), F32)
    return pl.pallas_call(
        write_kernel,
        out_shape=(
            jax.ShapeDtypeStruct((4, 8, 8192), F32), whole, whole, whole, whole
        ),
        in_specs=[vmem] * 6 + [hbm],
        out_specs=(hbm,) * 5,
        scratch_shapes=[
            words, pltpu.VMEM((N, 128), F32), pltpu.VMEM((4, 8, 8192), F32),
            table_smem, dma((9,)),
        ],
        compiler_params=pltpu.CompilerParams(vmem_limit_bytes=16 * 2**20),
    )(*mids, table)


def solution(mesh):
    owned = P(("replica", "fsdp"), None, None)
    return jax.shard_map(
        body,
        mesh=mesh,
        in_specs=(P("replica", "fsdp", None, None),) + (owned,) * 6 + (P(),),
        out_specs=(P("fsdp", "replica", None),) + (owned,) * 4,
        check_vma=False,
    )
```

```python
import functools

import jax
import jax.numpy as jnp
from jax import lax
from jax.experimental import pallas as pl
from jax.experimental.pallas import tpu as pltpu
from jax.sharding import PartitionSpec as P

MESH = pl.DeviceIdType.MESH
N = 128
B = 512
TINY = 1e-33
FAR_Z = (4, 3, 5, 2, 6, 1, 7, 0)
F32, BF16, I32 = jnp.float32, jnp.bfloat16, jnp.int32
CHUNKS = 4
WIDE = 8192 // CHUNKS


def far_x(plane):
    return jnp.where(plane == 0, 2, jnp.where(plane == 3, 0, 2 * plane - 1))


def turned(step, size, rep):
    return lax.rem(jnp.where(rep == 0, step, size - step), size)


def split(x):
    high = x.astype(BF16)
    return high, (x - high.astype(F32)).astype(BF16)


def dot3(a, b, dims=((1,), (0,))):
    one = functools.partial(
        lax.dot_general,
        dimension_numbers=(dims, ((), ())),
        preferred_element_type=F32,
    )
    return one(a[0], b[0]) + (one(a[0], b[1]) + one(a[1], b[0]))


def dot3_few(a, b):
    both = jnp.dot(
        jnp.concatenate(a, axis=0), b[0], preferred_element_type=F32
    )
    count = a[0].shape[0]
    cross = jnp.dot(a[0], b[1], preferred_element_type=F32)
    return both[:count] + (both[count:] + cross)


def pack(q):
    return (q[:, :256] << 16) | (q[:, 256:] & 0xFFFF)


def unpack(w):
    return w >> 16, (w << 16) >> 16


def rows(start, size=8):
    return pl.ds(pl.multiple_of(start, 8), size)


def step_kernel(
    g_hbm, l_hbm, r_hbm, m_hbm, v_hbm, lf_hbm, rf_hbm, table_hbm,
    back_words, back_scales, new_first, new_second, new_left, new_right,
    g, l, r, m, v, lf, rf, table,
    own, sib_out, sib_in, pieces, scales, out_words, out_scales, in_words, in_scales,
    blocks, lh, ll, lth, ltl, rh, rl, rth, rtl, bh, bl, wh, wl, ret_words, ret_scales,
    met, g_sem, in_sem, sib_send, sib_recv, fwd_send, fwd_recv, bwd_send, bwd_recv,
):
    rep = lax.axis_index("replica")
    me = lax.axis_index("fsdp")
    wides = [pl.ds(j * WIDE, WIDE) for j in range(CHUNKS)]
    loads = [
        pltpu.make_async_copy(g_hbm.at[0, :, :, w], g.at[:, :, w], g_sem.at[j])
        for j, w in enumerate(wides)
    ]
    pairs = (
        (table_hbm, table), (l_hbm.at[0], l), (r_hbm.at[0], r), (m_hbm.at[0], m),
        (v_hbm.at[0], v), (lf_hbm.at[0], lf), (rf_hbm.at[0], rf),
    )
    others = [
        pltpu.make_async_copy(a, b, in_sem.at[j]) for j, (a, b) in enumerate(pairs)
    ]
    for copy in loads:
        copy.start()

    x, y, z = me // 32, lax.rem(me // 8, 4), lax.rem(me, 8)
    line = [x * 32 + y * 8 + lax.rem(z + d, 8) for d in range(1, 8)]
    slab = [
        lax.rem(x + d // 4, 4) * 32 + lax.rem(y + d, 4) * 8 + z for d in range(1, 16)
    ]
    barrier = pltpu.get_barrier_semaphore()
    for peer in [(1 - rep, me)] + [(rep, q) for q in line + slab]:
        pl.semaphore_signal(barrier, inc=1, device_id=peer, device_id_type=MESH)
    for copy in others:
        copy.start()

    def part(c):
        cols = pl.ds(c * B, B)
        for pair in range(2):
            sent = []
            for i in (2 * pair, 2 * pair + 1):
                x = g[i, :, cols].astype(F32)
                low, high = x[:8], x[8:]
                own[i, :, cols] = jnp.where(rep == 0, low, high)
                sent.append(jnp.where(rep == 0, high, low))
            sib_out[pair, :, cols] = jnp.concatenate(sent, axis=0).astype(BF16)

    exchange = [
        pltpu.make_async_remote_copy(
            src_ref=sib_out.at[:, :, w],
            dst_ref=sib_in.at[:, :, w],
            send_sem=sib_send.at[j],
            recv_sem=sib_recv.at[j],
            device_id=(1 - rep, me),
            device_id_type=MESH,
        )
        for j, w in enumerate(wides)
    ]
    for j, copy in enumerate(loads):
        copy.wait()
        for c in range(j * 16 // CHUNKS, (j + 1) * 16 // CHUNKS):
            part(c)
        if j == 0:
            pl.semaphore_wait(barrier, 23)
        exchange[j].start()
        if j == 0:
            for q in line:
                pl.semaphore_signal(
                    met, inc=1, device_id=(rep, q), device_id_type=MESH
                )

    def code(c):
        cols = pl.ds(c * B, B)
        xs = []
        for pair in range(2):
            y = sib_in[pair, :, cols].astype(F32)
            xs.append(own[2 * pair, :, cols] + y[:8])
            xs.append(own[2 * pair + 1, :, cols] + y[8:])
        top = functools.reduce(jnp.maximum, [jnp.abs(x) for x in xs])
        top = jnp.maximum(jnp.max(top, axis=1, keepdims=True), TINY)
        inverse = 32767.0 / top
        for i, x in enumerate(xs):
            w = pack(jnp.round(x * inverse).astype(I32))
            for half in range(2):
                pieces[pl.ds(c * 8 + i * 2 + half, 8, stride=128), :] = w[
                    :, half * 128 : half * 128 + 128
                ]
        scales[pl.ds(c, 8, stride=16), :] = jnp.broadcast_to(
            top * (1.0 / 32767.0), (8, 128)
        )

    for j, copy in enumerate(exchange):
        copy.wait()
        for c in range(j * 16 // CHUNKS, (j + 1) * 16 // CHUNKS):
            code(c)

    ends = [lax.rem(z + turned(d, 8, rep), 8) for d in FAR_Z]

    def partners(block):
        at_y = lax.rem(y + turned(far_x(lax.rem(block, 4)), 4, rep), 4)
        at_x = lax.rem(x + turned(far_x(block // 4), 4, rep), 4)
        return [at_x * 32 + at_y * 8 + end for end in ends]

    def gather(block, found):
        stock = pieces.reshape(N, 8, 128)
        picked = []
        for q in found:
            k = table[rep, q]
            picked.append((stock[k], scales[pl.ds(k, 1), :]))
        for u, (word, scale) in enumerate(picked):
            out_words[rows(block * 64 + u * 8), :] = word
            out_scales[block * 8 + u] = scale

    def sends(words, lines, to_words, to_lines, send_sem, recv_sem, plane, forward):
        def one(block, found, count):
            for u, q in enumerate(found[:count]):
                slot = block * 8 + u if forward else q
                pltpu.make_async_remote_copy(
                    src_ref=words.at[rows(slot * 8)],
                    dst_ref=to_words.at[rows(me * 8)],
                    send_sem=send_sem.at[0],
                    recv_sem=recv_sem.at[0],
                    device_id=(rep, q),
                    device_id_type=MESH,
                ).start()
                pltpu.make_async_remote_copy(
                    src_ref=lines.at[slot],
                    dst_ref=to_lines.at[me],
                    send_sem=send_sem.at[1],
                    recv_sem=recv_sem.at[1],
                    device_id=(rep, q),
                    device_id_type=MESH,
                ).start()

        def whole(block, c, count=8):
            found = partners(block)
            if forward:
                gather(block, found)
            one(block, found, count)
            return c

        lax.fori_loop(plane * 4, min(plane * 4 + 4, 15), whole, 0)
        if plane == 3:
            whole(jnp.int32(15), 0, 7)

    others[0].wait()
    pl.semaphore_wait(met, 7)
    for plane in range(4):
        sends(
            out_words, out_scales, in_words, in_scales,
            fwd_send, fwd_recv.at[plane], plane, True,
        )
    in_words[rows(me * 8), :] = out_words[rows(8 * (N - 1)), :]
    in_scales[me] = out_scales[N - 1]

    def away(plane):
        return lax.rem(x + 4 - turned(far_x(plane), 4, rep), 4)

    for copy in others[1:]:
        copy.wait()
    for full, h, w in ((l, lh, ll), (r, rh, rl)):
        h[...], w[...] = split(full[...])
    rth[...], rtl[...] = split(r[...].T)
    for plane in range(4):
        cols = slice(plane * 128, plane * 128 + 128)
        lth[:, cols], ltl[:, cols] = split(l[rows(away(plane) * 128, 128), :].T)

    def arrived(sems, words, lines, count):
        pltpu.make_async_copy(
            words.at[rows(0, 8 * count)], words.at[rows(0, 8 * count)], sems.at[0]
        ).wait()
        pltpu.make_async_copy(
            lines.at[pl.ds(0, count)], lines.at[pl.ds(0, count)], sems.at[1]
        ).wait()

    upper = lax.broadcasted_iota(I32, (8, 128), 0) < 4

    def decode(j):
        scale = jnp.where(
            upper,
            jnp.broadcast_to(in_scales[2 * j], (8, 128)),
            jnp.broadcast_to(in_scales[2 * j + 1], (8, 128)),
        )
        for half in range(2):
            a, b = unpack(in_words[pl.ds(j * 16 + half, 8, stride=2), :])
            for q, col in ((a, half), (b, half + 2)):
                blocks[rows(j * 8), col * 128 : col * 128 + 128] = q.astype(F32) * scale

    for plane in range(4):
        arrived(fwd_recv.at[plane], in_words, in_scales, 31 if plane == 3 else 32)
        first = away(plane) * 16
        for j in range(16):
            decode(first + j)
        some, here = rows(first * 8, 128), slice(plane * 128, plane * 128 + 128)
        high, low = split(blocks[some, :])
        bh[some, :], bl[some, :] = high, low
        wh[here, :], wl[here, :] = split(
            dot3_few((high, low), (rh[...], rl[...]))
        )
        if plane == 2:
            new_first[...] = dot3(
                (lth[:, :384], ltl[:, :384]), (wh[:384, :], wl[:384, :])
            )
    tail = wh[384:, :]
    rotated = new_first[...] + (
        jnp.dot(
            jnp.concatenate([lth[:, 384:], ltl[:, 384:]], axis=1),
            jnp.concatenate([tail, tail], axis=0),
            preferred_element_type=F32,
        )
        + jnp.dot(lth[:, 384:], wl[384:, :], preferred_element_type=F32)
    )
    first = 0.95 * m[...] + 0.05 * rotated
    second = 0.95 * v[...] + 0.05 * rotated * rotated
    new_first[...] = first
    new_second[...] = second
    wh[...], wl[...] = split(first / (jnp.sqrt(second) + 1e-08))

    def encode(j, x):
        top = jnp.max(jnp.max(jnp.abs(x), axis=0, keepdims=True), axis=1, keepdims=True)
        top = jnp.maximum(top, TINY)
        w = pack(jnp.round(x * (32767.0 / top)).astype(I32))
        for half in range(2):
            ret_words[pl.ds(j * 16 + half, 8, stride=2), :] = w[
                :, half * 128 : half * 128 + 128
            ]
        scale = jnp.broadcast_to(top * (1.0 / 32767.0), (1, 128))
        ret_scales[2 * j] = scale
        ret_scales[2 * j + 1] = scale

    for plane in range(4):
        first = lax.rem(x + turned(far_x(plane), 4, rep), 4) * 16
        some = rows(first * 8, 128)
        part_left = split(dot3_few((lh[some, :], ll[some, :]), (wh[...], wl[...])))
        back = dot3_few(part_left, (rth[...], rtl[...]))
        for j in range(16):
            encode(first + j, back[j * 8 : j * 8 + 8, :])
        sends(
            ret_words, ret_scales, back_words, back_scales,
            bwd_send, bwd_recv, plane, False,
        )
    back_words[rows(me * 8), :] = ret_words[rows(me * 8), :]
    back_scales[me] = ret_scales[me]

    pair = (bh[...], bl[...])
    new_left[...] = 0.95 * lf[...] + 0.05 * dot3(pair, pair, ((1,), (1,)))
    new_right[...] = 0.95 * rf[...] + 0.05 * dot3(pair, pair, ((0,), (0,)))

    arrived(fwd_send, out_words, out_scales, N - 1)
    arrived(bwd_send, ret_words, ret_scales, N - 1)
    arrived(bwd_recv, back_words, back_scales, N - 1)


def write_kernel(
    words, lines, first, second, left, right, table_hbm,
    update_hbm, first_hbm, second_hbm, left_hbm, right_hbm,
    pieces, scales, update, table, sems,
):
    rep = lax.axis_index("replica")
    fetch = pltpu.make_async_copy(table_hbm, table, sems.at[8])
    fetch.start()
    pairs = ((first, first_hbm), (second, second_hbm), (left, left_hbm), (right, right_hbm))
    copies = [
        pltpu.make_async_copy(a, b.at[0], sems.at[j]) for j, (a, b) in enumerate(pairs)
    ]
    for copy in copies:
        copy.start()
    fetch.wait()

    def place(q, c):
        k = table[rep, q]
        pieces[rows(k * 8), :] = words[rows(q * 8), :]
        scales[pl.ds(k, 1), :] = lines[q]
        return c

    lax.fori_loop(0, N, place, 0, unroll=8)

    def decode(c):
        scale = scales[pl.ds(c, 8, stride=16), :]
        for i in range(4):
            for half in range(2):
                w = pieces[pl.ds(c * 8 + i * 2 + half, 8, stride=128), :]
                for q, col in zip(unpack(w), (half, half + 2)):
                    cols = pl.ds(c * B + col * 128, 128)
                    update[i, :, cols] = q.astype(F32) * scale

    for j in range(CHUNKS):
        for c in range(j * 16 // CHUNKS, (j + 1) * 16 // CHUNKS):
            decode(c)
        w = pl.ds(j * WIDE, WIDE)
        copies.append(
            pltpu.make_async_copy(
                update.at[:, :, w], update_hbm.at[:, :, w], sems.at[4 + j]
            )
        )
        copies[-1].start()
    for copy in copies:
        copy.wait()


def body(grad_parts, left_basis, right_basis, first, second, left, right, table):
    hbm = pl.BlockSpec(memory_space=pltpu.HBM)
    vmem = pl.BlockSpec(memory_space=pltpu.VMEM)
    table_smem = pltpu.SMEM((2, N), I32)
    square = jax.ShapeDtypeStruct((B, B), F32)
    halves = [pltpu.VMEM((B, B), BF16)] * 12
    words, lines = pltpu.VMEM((N * 8, 128), I32), pltpu.VMEM((N, 1, 128), F32)
    dma = pltpu.SemaphoreType.DMA
    mids = pl.pallas_call(
        step_kernel,
        out_shape=(
            jax.ShapeDtypeStruct((N * 8, 128), I32),
            jax.ShapeDtypeStruct((N, 1, 128), F32),
            square, square, square, square,
        ),
        in_specs=[hbm] * 8,
        out_specs=(vmem,) * 6,
        scratch_shapes=[
            pltpu.VMEM((4, 16, 8192), BF16),
            *[pltpu.VMEM((B, B), F32)] * 6,
            table_smem,
            pltpu.VMEM((4, 8, 8192), F32),
            pltpu.VMEM((2, 16, 8192), BF16),
            pltpu.VMEM((2, 16, 8192), BF16),
            words, pltpu.VMEM((N, 128), F32), words, lines, words, lines,
            pltpu.VMEM((B, B), F32),
            *halves,
            words, lines,
            pltpu.SemaphoreType.REGULAR,
            dma((CHUNKS,)), dma((7,)), dma((CHUNKS,)), dma((CHUNKS,)),
            dma((2,)), dma((4, 2)), dma((2,)), dma((2,)),
        ],
        compiler_params=pltpu.CompilerParams(
            collective_id=0, has_side_effects=True, vmem_limit_bytes=49 * 2**20
        ),
    )(grad_parts, left_basis, right_basis, first, second, left, right, table)
    whole = jax.ShapeDtypeStruct((1, B, B), F32)
    return pl.pallas_call(
        write_kernel,
        out_shape=(
            jax.ShapeDtypeStruct((4, 8, 8192), F32), whole, whole, whole, whole
        ),
        in_specs=[vmem] * 6 + [hbm],
        out_specs=(hbm,) * 5,
        scratch_shapes=[
            words, pltpu.VMEM((N, 128), F32), pltpu.VMEM((4, 8, 8192), F32),
            table_smem, dma((9,)),
        ],
        compiler_params=pltpu.CompilerParams(vmem_limit_bytes=16 * 2**20),
    )(*mids, table)


def solution(mesh):
    owned = P(("replica", "fsdp"), None, None)
    return jax.shard_map(
        body,
        mesh=mesh,
        in_specs=(P("replica", "fsdp", None, None),) + (owned,) * 6 + (P(),),
        out_specs=(P("fsdp", "replica", None),) + (owned,) * 4,
        check_vma=False,
    )
```

```python
import functools
import math

import jax
import jax.numpy as jnp
from jax import lax
from jax.experimental import pallas as pl
from jax.experimental.pallas import tpu as pltpu
from jax.sharding import PartitionSpec as P

MESH = pl.DeviceIdType.MESH
N = 128
B = 512
TINY = 1e-33
MOST, LEAST = math.log2(3.0), -126.0
COARSE = 24.0
FINE = (32767 - COARSE * (MOST - 28 - LEAST)) / 28
FAR_Z = (4, 3, 5, 2, 6, 1, 7, 0)
F32, BF16, I32 = jnp.float32, jnp.bfloat16, jnp.int32
CHUNKS = 4
WIDE = 8192 // CHUNKS


def far_x(plane):
    return jnp.where(plane == 0, 2, jnp.where(plane == 3, 0, 2 * plane - 1))


def turned(step, size, rep):
    return lax.rem(jnp.where(rep == 0, step, size - step), size)


def split(x):
    high = x.astype(BF16)
    return high, (x - high.astype(F32)).astype(BF16)


def dot3(a, b, dims=((1,), (0,))):
    one = functools.partial(
        lax.dot_general,
        dimension_numbers=(dims, ((), ())),
        preferred_element_type=F32,
    )
    return one(a[0], b[0]) + (one(a[0], b[1]) + one(a[1], b[0]))


def dot3_few(a, b):
    both = jnp.dot(
        jnp.concatenate(a, axis=0), b[0], preferred_element_type=F32
    )
    count = a[0].shape[0]
    cross = jnp.dot(a[0], b[1], preferred_element_type=F32)
    return both[:count] + (both[count:] + cross)


def log_code(x):
    size = jnp.log2(jnp.maximum(jnp.abs(x), 2.0**LEAST))
    code = jnp.maximum(FINE * (size - MOST) + 32767.0, COARSE * (size - LEAST))
    code = jnp.round(code).astype(I32)
    return jnp.where(x < 0, -code, code)


def log_value(code):
    steps = jnp.abs(code).astype(F32)
    size = jnp.minimum(
        (steps - 32767.0) * (1 / FINE) + MOST, steps * (1 / COARSE) + LEAST
    )
    size = jnp.exp2(size)
    return jnp.where(code == 0, 0.0, jnp.where(code < 0, -size, size))


def pack(q):
    return (q[:, :256] << 16) | (q[:, 256:] & 0xFFFF)


def unpack(w):
    return w >> 16, (w << 16) >> 16


def rows(start, size=8):
    return pl.ds(pl.multiple_of(start, 8), size)


def step_kernel(
    g_hbm, l_hbm, r_hbm, m_hbm, v_hbm, lf_hbm, rf_hbm, table_hbm,
    back_words, back_scales, new_first, new_second, new_left, new_right,
    g, l, r, m, v, lf, rf, table,
    own, sib_out, sib_in, pieces, out_words, in_words,
    blocks, lh, ll, lth, ltl, rh, rl, rth, rtl, bh, bl, wh, wl, ret_words, ret_scales,
    met, g_sem, in_sem, sib_send, sib_recv, fwd_send, fwd_recv, bwd_send, bwd_recv,
):
    rep = lax.axis_index("replica")
    me = lax.axis_index("fsdp")
    wides = [pl.ds(j * WIDE, WIDE) for j in range(CHUNKS)]
    loads = [
        pltpu.make_async_copy(g_hbm.at[0, :, :, w], g.at[:, :, w], g_sem.at[j])
        for j, w in enumerate(wides)
    ]
    pairs = (
        (table_hbm, table), (l_hbm.at[0], l), (r_hbm.at[0], r), (m_hbm.at[0], m),
        (v_hbm.at[0], v), (lf_hbm.at[0], lf), (rf_hbm.at[0], rf),
    )
    others = [
        pltpu.make_async_copy(a, b, in_sem.at[j]) for j, (a, b) in enumerate(pairs)
    ]
    for copy in loads:
        copy.start()

    x, y, z = me // 32, lax.rem(me // 8, 4), lax.rem(me, 8)
    line = [x * 32 + y * 8 + lax.rem(z + d, 8) for d in range(1, 8)]
    slab = [
        lax.rem(x + d // 4, 4) * 32 + lax.rem(y + d, 4) * 8 + z for d in range(1, 16)
    ]
    barrier = pltpu.get_barrier_semaphore()
    for peer in [(1 - rep, me)] + [(rep, q) for q in line + slab]:
        pl.semaphore_signal(barrier, inc=1, device_id=peer, device_id_type=MESH)
    for copy in others:
        copy.start()

    def part(c):
        cols = pl.ds(c * B, B)
        for pair in range(2):
            sent = []
            for i in (2 * pair, 2 * pair + 1):
                x = g[i, :, cols].astype(F32)
                low, high = x[:8], x[8:]
                own[i, :, cols] = jnp.where(rep == 0, low, high)
                sent.append(jnp.where(rep == 0, high, low))
            sib_out[pair, :, cols] = jnp.concatenate(sent, axis=0).astype(BF16)

    exchange = [
        pltpu.make_async_remote_copy(
            src_ref=sib_out.at[:, :, w],
            dst_ref=sib_in.at[:, :, w],
            send_sem=sib_send.at[j],
            recv_sem=sib_recv.at[j],
            device_id=(1 - rep, me),
            device_id_type=MESH,
        )
        for j, w in enumerate(wides)
    ]
    for j, copy in enumerate(loads):
        copy.wait()
        for c in range(j * 16 // CHUNKS, (j + 1) * 16 // CHUNKS):
            part(c)
        if j == 0:
            pl.semaphore_wait(barrier, 23)
        exchange[j].start()
        if j == 0:
            for q in line:
                pl.semaphore_signal(
                    met, inc=1, device_id=(rep, q), device_id_type=MESH
                )

    def code(c):
        cols = pl.ds(c * B, B)
        xs = []
        for pair in range(2):
            y = sib_in[pair, :, cols].astype(F32)
            xs.append(own[2 * pair, :, cols] + y[:8])
            xs.append(own[2 * pair + 1, :, cols] + y[8:])
        for i, x in enumerate(xs):
            w = pack(log_code(x))
            for half in range(2):
                pieces[pl.ds(c * 8 + i * 2 + half, 8, stride=128), :] = w[
                    :, half * 128 : half * 128 + 128
                ]

    for j, copy in enumerate(exchange):
        copy.wait()
        for c in range(j * 16 // CHUNKS, (j + 1) * 16 // CHUNKS):
            code(c)

    ends = [lax.rem(z + turned(d, 8, rep), 8) for d in FAR_Z]

    def first_of(block):
        at_y = lax.rem(y + turned(far_x(lax.rem(block, 4)), 4, rep), 4)
        at_x = lax.rem(x + turned(far_x(block // 4), 4, rep), 4)
        return at_x * 32 + at_y * 8

    def partners(block):
        return [first_of(block) + end for end in ends]

    def gather(block, found):
        stock = pieces.reshape(N, 8, 128)
        picked = []
        for q in found:
            k = table[rep, q]
            picked.append(stock[k])
        for u, word in enumerate(picked):
            out_words[rows(block * 64 + u * 8), :] = word

    def sends(words, lines, to_words, to_lines, send_sem, recv_sem, begin, end, forward):
        def one(block, found, count):
            for u, q in enumerate(found[:count]):
                slot = block * 8 + u if forward else q
                pltpu.make_async_remote_copy(
                    src_ref=words.at[rows(slot * 8)],
                    dst_ref=to_words.at[rows(me * 8)],
                    send_sem=send_sem.at[0],
                    recv_sem=recv_sem.at[0],
                    device_id=(rep, q),
                    device_id_type=MESH,
                ).start()
                if forward:
                    continue
                pltpu.make_async_remote_copy(
                    src_ref=lines.at[slot],
                    dst_ref=to_lines.at[me],
                    send_sem=send_sem.at[1],
                    recv_sem=recv_sem.at[1],
                    device_id=(rep, q),
                    device_id_type=MESH,
                ).start()

        def whole(block, c, count=8):
            found = partners(block)
            if forward:
                gather(block, found)
            one(block, found, count)
            return c

        lax.fori_loop(begin, min(end, 15), whole, 0)
        if end == 16:
            whole(jnp.int32(15), 0, 7)

    others[0].wait()
    pl.semaphore_wait(met, 7)
    for plane in range(4):
        sends(
            out_words, None, in_words, None,
            fwd_send, fwd_recv.at[plane], plane * 4, plane * 4 + 4, True,
        )
    in_words[rows(me * 8), :] = out_words[rows(8 * (N - 1)), :]

    def away(plane):
        return lax.rem(x + 4 - turned(far_x(plane), 4, rep), 4)

    for copy in others[1:]:
        copy.wait()
    for full, h, w in ((l, lh, ll), (r, rh, rl)):
        h[...], w[...] = split(full[...])
    rth[...], rtl[...] = split(r[...].T)
    for plane in range(4):
        cols = slice(plane * 128, plane * 128 + 128)
        lth[:, cols], ltl[:, cols] = split(l[rows(away(plane) * 128, 128), :].T)

    def arrived(sems, words, lines, count):
        pltpu.make_async_copy(
            words.at[rows(0, 8 * count)], words.at[rows(0, 8 * count)], sems.at[0]
        ).wait()
        if lines is None:
            return
        pltpu.make_async_copy(
            lines.at[pl.ds(0, count)], lines.at[pl.ds(0, count)], sems.at[1]
        ).wait()

    def decode(j):
        for half in range(2):
            a, b = unpack(in_words[pl.ds(j * 16 + half, 8, stride=2), :])
            for q, col in ((a, half), (b, half + 2)):
                blocks[rows(j * 8), col * 128 : col * 128 + 128] = log_value(q)

    for plane in range(4):
        arrived(fwd_recv.at[plane], in_words, None, 31 if plane == 3 else 32)
        first = away(plane) * 16
        for j in range(16):
            decode(first + j)
        some, here = rows(first * 8, 128), slice(plane * 128, plane * 128 + 128)
        high, low = split(blocks[some, :])
        bh[some, :], bl[some, :] = high, low
        wh[here, :], wl[here, :] = split(
            dot3_few((high, low), (rh[...], rl[...]))
        )
        if plane == 2:
            new_first[...] = dot3(
                (lth[:, :384], ltl[:, :384]), (wh[:384, :], wl[:384, :])
            )
    tail = wh[384:, :]
    rotated = new_first[...] + (
        jnp.dot(
            jnp.concatenate([lth[:, 384:], ltl[:, 384:]], axis=1),
            jnp.concatenate([tail, tail], axis=0),
            preferred_element_type=F32,
        )
        + jnp.dot(lth[:, 384:], wl[384:, :], preferred_element_type=F32)
    )
    first = 0.95 * m[...] + 0.05 * rotated
    second = 0.95 * v[...] + 0.05 * rotated * rotated
    new_first[...] = first
    new_second[...] = second
    wh[...], wl[...] = split(first / (jnp.sqrt(second) + 1e-08))

    def encode(j, x):
        top = jnp.max(jnp.max(jnp.abs(x), axis=0, keepdims=True), axis=1, keepdims=True)
        top = jnp.maximum(top, TINY)
        w = pack(jnp.round(x * (32767.0 / top)).astype(I32))
        for half in range(2):
            ret_words[pl.ds(j * 16 + half, 8, stride=2), :] = w[
                :, half * 128 : half * 128 + 128
            ]
        scale = jnp.broadcast_to(top * (1.0 / 32767.0), (1, 128))
        ret_scales[2 * j] = scale
        ret_scales[2 * j + 1] = scale

    for begin, end in ((0, 2), (2, 4), (4, 8), (8, 12), (12, 16)):
        firsts = [first_of(block) for block in range(begin, end)]
        some = [
            jnp.concatenate([half[rows(first * 4, 32), :] for first in firsts], axis=0)
            for half in (lh, ll)
        ]
        part_left = split(dot3_few(some, (wh[...], wl[...])))
        back = dot3_few(part_left, (rth[...], rtl[...]))
        for i in range(4 * (end - begin)):
            j = lax.div(firsts[i // 4], 2) + i % 4
            encode(j, back[i * 8 : i * 8 + 8, :])
        sends(
            ret_words, ret_scales, back_words, back_scales,
            bwd_send, bwd_recv, begin, end, False,
        )
    back_words[rows(me * 8), :] = ret_words[rows(me * 8), :]
    back_scales[me] = ret_scales[me]

    pair = (bh[...], bl[...])
    new_left[...] = 0.95 * lf[...] + 0.05 * dot3(pair, pair, ((1,), (1,)))
    new_right[...] = 0.95 * rf[...] + 0.05 * dot3(pair, pair, ((0,), (0,)))

    arrived(fwd_send, out_words, None, N - 1)
    arrived(bwd_send, ret_words, ret_scales, N - 1)
    arrived(bwd_recv, back_words, back_scales, N - 1)


def write_kernel(
    words, lines, first, second, left, right, table_hbm,
    update_hbm, first_hbm, second_hbm, left_hbm, right_hbm,
    pieces, scales, update, table, sems,
):
    rep = lax.axis_index("replica")
    fetch = pltpu.make_async_copy(table_hbm, table, sems.at[8])
    fetch.start()
    pairs = ((first, first_hbm), (second, second_hbm), (left, left_hbm), (right, right_hbm))
    copies = [
        pltpu.make_async_copy(a, b.at[0], sems.at[j]) for j, (a, b) in enumerate(pairs)
    ]
    for copy in copies:
        copy.start()
    fetch.wait()

    def place(q, c):
        k = table[rep, q]
        pieces[rows(k * 8), :] = words[rows(q * 8), :]
        scales[pl.ds(k, 1), :] = lines[q]
        return c

    lax.fori_loop(0, N, place, 0, unroll=8)

    def decode(c):
        scale = scales[pl.ds(c, 8, stride=16), :]
        for i in range(4):
            for half in range(2):
                w = pieces[pl.ds(c * 8 + i * 2 + half, 8, stride=128), :]
                for q, col in zip(unpack(w), (half, half + 2)):
                    cols = pl.ds(c * B + col * 128, 128)
                    update[i, :, cols] = q.astype(F32) * scale

    for j in range(CHUNKS):
        for c in range(j * 16 // CHUNKS, (j + 1) * 16 // CHUNKS):
            decode(c)
        w = pl.ds(j * WIDE, WIDE)
        copies.append(
            pltpu.make_async_copy(
                update.at[:, :, w], update_hbm.at[:, :, w], sems.at[4 + j]
            )
        )
        copies[-1].start()
    for copy in copies:
        copy.wait()


def body(grad_parts, left_basis, right_basis, first, second, left, right, table):
    hbm = pl.BlockSpec(memory_space=pltpu.HBM)
    vmem = pl.BlockSpec(memory_space=pltpu.VMEM)
    table_smem = pltpu.SMEM((2, N), I32)
    square = jax.ShapeDtypeStruct((B, B), F32)
    halves = [pltpu.VMEM((B, B), BF16)] * 12
    words, lines = pltpu.VMEM((N * 8, 128), I32), pltpu.VMEM((N, 1, 128), F32)
    dma = pltpu.SemaphoreType.DMA
    mids = pl.pallas_call(
        step_kernel,
        out_shape=(
            jax.ShapeDtypeStruct((N * 8, 128), I32),
            jax.ShapeDtypeStruct((N, 1, 128), F32),
            square, square, square, square,
        ),
        in_specs=[hbm] * 8,
        out_specs=(vmem,) * 6,
        scratch_shapes=[
            pltpu.VMEM((4, 16, 8192), BF16),
            *[pltpu.VMEM((B, B), F32)] * 6,
            table_smem,
            pltpu.VMEM((4, 8, 8192), F32),
            pltpu.VMEM((2, 16, 8192), BF16),
            pltpu.VMEM((2, 16, 8192), BF16),
            words, words, words,
            pltpu.VMEM((B, B), F32),
            *halves,
            words, lines,
            pltpu.SemaphoreType.REGULAR,
            dma((CHUNKS,)), dma((7,)), dma((CHUNKS,)), dma((CHUNKS,)),
            dma((1,)), dma((4, 1)), dma((2,)), dma((2,)),
        ],
        compiler_params=pltpu.CompilerParams(
            collective_id=0, has_side_effects=True, vmem_limit_bytes=49 * 2**20
        ),
    )(grad_parts, left_basis, right_basis, first, second, left, right, table)
    whole = jax.ShapeDtypeStruct((1, B, B), F32)
    return pl.pallas_call(
        write_kernel,
        out_shape=(
            jax.ShapeDtypeStruct((4, 8, 8192), F32), whole, whole, whole, whole
        ),
        in_specs=[vmem] * 6 + [hbm],
        out_specs=(hbm,) * 5,
        scratch_shapes=[
            words, pltpu.VMEM((N, 128), F32), pltpu.VMEM((4, 8, 8192), F32),
            table_smem, dma((9,)),
        ],
        compiler_params=pltpu.CompilerParams(vmem_limit_bytes=16 * 2**20),
    )(*mids, table)


def solution(mesh):
    owned = P(("replica", "fsdp"), None, None)
    return jax.shard_map(
        body,
        mesh=mesh,
        in_specs=(P("replica", "fsdp", None, None),) + (owned,) * 6 + (P(),),
        out_specs=(P("fsdp", "replica", None),) + (owned,) * 4,
        check_vma=False,
    )
```

```python
import functools
import math

import jax
import jax.numpy as jnp
from jax import lax
from jax.experimental import pallas as pl
from jax.experimental.pallas import tpu as pltpu
from jax.sharding import PartitionSpec as P

MESH = pl.DeviceIdType.MESH
N = 128
B = 512
TINY = 1e-33
MOST, LEAST = math.log2(3.0), -126.0
COARSE = 24.0
FINE = (32767 - COARSE * (MOST - 28 - LEAST)) / 28
FAR_Z = (4, 3, 5, 2, 6, 1, 7, 0)
F32, BF16, I32 = jnp.float32, jnp.bfloat16, jnp.int32
CHUNKS = 4
WIDE = 8192 // CHUNKS


def far_x(plane):
    return jnp.where(plane == 0, 2, jnp.where(plane == 3, 0, 2 * plane - 1))


def near_x(plane):
    return jnp.where(plane == 3, 0, plane + 1)


def turned(step, size, rep):
    return lax.rem(jnp.where(rep == 0, step, size - step), size)


def split(x):
    high = x.astype(BF16)
    return high, (x - high.astype(F32)).astype(BF16)


def dot3(a, b, dims=((1,), (0,))):
    one = functools.partial(
        lax.dot_general,
        dimension_numbers=(dims, ((), ())),
        preferred_element_type=F32,
    )
    return one(a[0], b[0]) + (one(a[0], b[1]) + one(a[1], b[0]))


def dot3_few(a, b):
    both = jnp.dot(
        jnp.concatenate(a, axis=0), b[0], preferred_element_type=F32
    )
    count = a[0].shape[0]
    cross = jnp.dot(a[0], b[1], preferred_element_type=F32)
    return both[:count] + (both[count:] + cross)


def log_code(x):
    size = jnp.log2(jnp.maximum(jnp.abs(x), 2.0**LEAST))
    code = jnp.maximum(FINE * (size - MOST) + 32767.0, COARSE * (size - LEAST))
    code = jnp.round(code).astype(I32)
    return jnp.where(x < 0, -code, code)


def log_value(code):
    steps = jnp.abs(code).astype(F32)
    size = jnp.minimum(
        (steps - 32767.0) * (1 / FINE) + MOST, steps * (1 / COARSE) + LEAST
    )
    size = jnp.exp2(size)
    return jnp.where(code == 0, 0.0, jnp.where(code < 0, -size, size))


def pack(q):
    return (q[:, :256] << 16) | (q[:, 256:] & 0xFFFF)


def unpack(w):
    return w >> 16, (w << 16) >> 16


def rows(start, size=8):
    return pl.ds(pl.multiple_of(start, 8), size)


def step_kernel(
    g_hbm, l_hbm, r_hbm, m_hbm, v_hbm, lf_hbm, rf_hbm, table_hbm,
    back_words, back_scales, new_first, new_second, new_left, new_right,
    g, l, r, m, v, lf, rf, table,
    own, sib_out, sib_in, pieces, out_words, in_words,
    blocks, lh, ll, lth, ltl, rh, rl, rth, rtl, bh, bl, wh, wl, ret_words, ret_scales,
    met, g_sem, in_sem, sib_send, sib_recv, fwd_send, fwd_recv, bwd_send, bwd_recv,
):
    rep = lax.axis_index("replica")
    me = lax.axis_index("fsdp")
    wides = [pl.ds(j * WIDE, WIDE) for j in range(CHUNKS)]
    loads = [
        pltpu.make_async_copy(g_hbm.at[0, :, :, w], g.at[:, :, w], g_sem.at[j])
        for j, w in enumerate(wides)
    ]
    pairs = (
        (table_hbm, table), (l_hbm.at[0], l), (r_hbm.at[0], r), (m_hbm.at[0], m),
        (v_hbm.at[0], v), (lf_hbm.at[0], lf), (rf_hbm.at[0], rf),
    )
    others = [
        pltpu.make_async_copy(a, b, in_sem.at[j]) for j, (a, b) in enumerate(pairs)
    ]
    for copy in loads:
        copy.start()

    x, y, z = me // 32, lax.rem(me // 8, 4), lax.rem(me, 8)
    line = [x * 32 + y * 8 + lax.rem(z + d, 8) for d in range(1, 8)]
    slab = [
        lax.rem(x + d // 4, 4) * 32 + lax.rem(y + d, 4) * 8 + z for d in range(1, 16)
    ]
    barrier = pltpu.get_barrier_semaphore()
    for peer in [(1 - rep, me)] + [(rep, q) for q in line + slab]:
        pl.semaphore_signal(barrier, inc=1, device_id=peer, device_id_type=MESH)
    for copy in others:
        copy.start()

    def part(c):
        cols = pl.ds(c * B, B)
        for pair in range(2):
            sent = []
            for i in (2 * pair, 2 * pair + 1):
                x = g[i, :, cols].astype(F32)
                low, high = x[:8], x[8:]
                own[i, :, cols] = jnp.where(rep == 0, low, high)
                sent.append(jnp.where(rep == 0, high, low))
            sib_out[pair, :, cols] = jnp.concatenate(sent, axis=0).astype(BF16)

    exchange = [
        pltpu.make_async_remote_copy(
            src_ref=sib_out.at[:, :, w],
            dst_ref=sib_in.at[:, :, w],
            send_sem=sib_send.at[j],
            recv_sem=sib_recv.at[j],
            device_id=(1 - rep, me),
            device_id_type=MESH,
        )
        for j, w in enumerate(wides)
    ]
    for j, copy in enumerate(loads):
        copy.wait()
        for c in range(j * 16 // CHUNKS, (j + 1) * 16 // CHUNKS):
            part(c)
        if j == 0:
            pl.semaphore_wait(barrier, 23)
        exchange[j].start()
        if j == 0:
            for q in line:
                pl.semaphore_signal(
                    met, inc=1, device_id=(rep, q), device_id_type=MESH
                )

    def code(c):
        cols = pl.ds(c * B, B)
        xs = []
        for pair in range(2):
            y = sib_in[pair, :, cols].astype(F32)
            xs.append(own[2 * pair, :, cols] + y[:8])
            xs.append(own[2 * pair + 1, :, cols] + y[8:])
        for i, x in enumerate(xs):
            w = pack(log_code(x))
            for half in range(2):
                pieces[pl.ds(c * 8 + i * 2 + half, 8, stride=128), :] = w[
                    :, half * 128 : half * 128 + 128
                ]

    for j, copy in enumerate(exchange):
        copy.wait()
        for c in range(j * 16 // CHUNKS, (j + 1) * 16 // CHUNKS):
            code(c)

    ends = [lax.rem(z + turned(d, 8, rep), 8) for d in FAR_Z]

    def first_of(block):
        at_y = lax.rem(y + turned(far_x(lax.rem(block, 4)), 4, rep), 4)
        at_x = lax.rem(x + turned(near_x(block // 4), 4, rep), 4)
        return at_x * 32 + at_y * 8

    def partners(block):
        return [first_of(block) + end for end in ends]

    def gather(block, found):
        stock = pieces.reshape(N, 8, 128)
        picked = []
        for q in found:
            k = table[rep, q]
            picked.append(stock[k])
        for u, word in enumerate(picked):
            out_words[rows(block * 64 + u * 8), :] = word

    def sends(words, lines, to_words, to_lines, send_sem, recv_sem, begin, end, forward):
        def one(block, found, count):
            for u, q in enumerate(found[:count]):
                slot = block * 8 + u if forward else q
                pltpu.make_async_remote_copy(
                    src_ref=words.at[rows(slot * 8)],
                    dst_ref=to_words.at[rows(me * 8)],
                    send_sem=send_sem.at[0],
                    recv_sem=recv_sem.at[0],
                    device_id=(rep, q),
                    device_id_type=MESH,
                ).start()
                if forward:
                    continue
                pltpu.make_async_remote_copy(
                    src_ref=lines.at[slot],
                    dst_ref=to_lines.at[me],
                    send_sem=send_sem.at[1],
                    recv_sem=recv_sem.at[1],
                    device_id=(rep, q),
                    device_id_type=MESH,
                ).start()

        def whole(block, c, count=8):
            found = partners(block)
            if forward:
                gather(block, found)
            one(block, found, count)
            return c

        lax.fori_loop(begin, min(end, 15), whole, 0)
        if end == 16:
            whole(jnp.int32(15), 0, 7)

    others[0].wait()
    pl.semaphore_wait(met, 7)
    for plane in range(4):
        sends(
            out_words, None, in_words, None,
            fwd_send, fwd_recv.at[plane], plane * 4, plane * 4 + 4, True,
        )
    in_words[rows(me * 8), :] = out_words[rows(8 * (N - 1)), :]

    def away(plane):
        return lax.rem(x + 4 - turned(near_x(plane), 4, rep), 4)

    for copy in others[1:]:
        copy.wait()
    for full, h, w in ((l, lh, ll), (r, rh, rl)):
        h[...], w[...] = split(full[...])
    rth[...], rtl[...] = split(r[...].T)
    for plane in range(4):
        cols = slice(plane * 128, plane * 128 + 128)
        lth[:, cols], ltl[:, cols] = split(l[rows(away(plane) * 128, 128), :].T)

    def arrived(sems, words, lines, count):
        pltpu.make_async_copy(
            words.at[rows(0, 8 * count)], words.at[rows(0, 8 * count)], sems.at[0]
        ).wait()
        if lines is None:
            return
        pltpu.make_async_copy(
            lines.at[pl.ds(0, count)], lines.at[pl.ds(0, count)], sems.at[1]
        ).wait()

    def decode(j):
        for half in range(2):
            a, b = unpack(in_words[pl.ds(j * 16 + half, 8, stride=2), :])
            for q, col in ((a, half), (b, half + 2)):
                blocks[rows(j * 8), col * 128 : col * 128 + 128] = log_value(q)

    for plane in range(4):
        arrived(fwd_recv.at[plane], in_words, None, 31 if plane == 3 else 32)
        first = away(plane) * 16
        for j in range(16):
            decode(first + j)
        some, here = rows(first * 8, 128), slice(plane * 128, plane * 128 + 128)
        high, low = split(blocks[some, :])
        bh[some, :], bl[some, :] = high, low
        wh[here, :], wl[here, :] = split(
            dot3_few((high, low), (rh[...], rl[...]))
        )
        if plane == 2:
            new_first[...] = dot3(
                (lth[:, :384], ltl[:, :384]), (wh[:384, :], wl[:384, :])
            )
    tail = wh[384:, :]
    rotated = new_first[...] + (
        jnp.dot(
            jnp.concatenate([lth[:, 384:], ltl[:, 384:]], axis=1),
            jnp.concatenate([tail, tail], axis=0),
            preferred_element_type=F32,
        )
        + jnp.dot(lth[:, 384:], wl[384:, :], preferred_element_type=F32)
    )
    first = 0.95 * m[...] + 0.05 * rotated
    second = 0.95 * v[...] + 0.05 * rotated * rotated
    new_first[...] = first
    new_second[...] = second
    wh[...], wl[...] = split(first / (jnp.sqrt(second) + 1e-08))

    def encode(j, x):
        top = jnp.max(jnp.max(jnp.abs(x), axis=0, keepdims=True), axis=1, keepdims=True)
        top = jnp.maximum(top, TINY)
        w = pack(jnp.round(x * (32767.0 / top)).astype(I32))
        for half in range(2):
            ret_words[pl.ds(j * 16 + half, 8, stride=2), :] = w[
                :, half * 128 : half * 128 + 128
            ]
        scale = jnp.broadcast_to(top * (1.0 / 32767.0), (1, 128))
        ret_scales[2 * j] = scale
        ret_scales[2 * j + 1] = scale

    for begin, end in ((0, 2), (2, 4), (4, 8), (8, 12), (12, 16)):
        firsts = [first_of(block) for block in range(begin, end)]
        some = [
            jnp.concatenate([half[rows(first * 4, 32), :] for first in firsts], axis=0)
            for half in (lh, ll)
        ]
        part_left = split(dot3_few(some, (wh[...], wl[...])))
        back = dot3_few(part_left, (rth[...], rtl[...]))
        for i in range(4 * (end - begin)):
            j = lax.div(firsts[i // 4], 2) + i % 4
            encode(j, back[i * 8 : i * 8 + 8, :])
        sends(
            ret_words, ret_scales, back_words, back_scales,
            bwd_send, bwd_recv, begin, end, False,
        )
    back_words[rows(me * 8), :] = ret_words[rows(me * 8), :]
    back_scales[me] = ret_scales[me]

    pair = (bh[...], bl[...])
    new_left[...] = 0.95 * lf[...] + 0.05 * dot3(pair, pair, ((1,), (1,)))
    new_right[...] = 0.95 * rf[...] + 0.05 * dot3(pair, pair, ((0,), (0,)))

    arrived(fwd_send, out_words, None, N - 1)
    arrived(bwd_send, ret_words, ret_scales, N - 1)
    arrived(bwd_recv, back_words, back_scales, N - 1)


def write_kernel(
    words, lines, first, second, left, right, table_hbm,
    update_hbm, first_hbm, second_hbm, left_hbm, right_hbm,
    pieces, scales, update, table, sems,
):
    rep = lax.axis_index("replica")
    fetch = pltpu.make_async_copy(table_hbm, table, sems.at[8])
    fetch.start()
    pairs = ((first, first_hbm), (second, second_hbm), (left, left_hbm), (right, right_hbm))
    copies = [
        pltpu.make_async_copy(a, b.at[0], sems.at[j]) for j, (a, b) in enumerate(pairs)
    ]
    for copy in copies:
        copy.start()
    fetch.wait()

    def place(q, c):
        k = table[rep, q]
        pieces[rows(k * 8), :] = words[rows(q * 8), :]
        scales[pl.ds(k, 1), :] = lines[q]
        return c

    lax.fori_loop(0, N, place, 0, unroll=8)

    def decode(c):
        scale = scales[pl.ds(c, 8, stride=16), :]
        for i in range(4):
            for half in range(2):
                w = pieces[pl.ds(c * 8 + i * 2 + half, 8, stride=128), :]
                for q, col in zip(unpack(w), (half, half + 2)):
                    cols = pl.ds(c * B + col * 128, 128)
                    update[i, :, cols] = q.astype(F32) * scale

    for j in range(CHUNKS):
        for c in range(j * 16 // CHUNKS, (j + 1) * 16 // CHUNKS):
            decode(c)
        w = pl.ds(j * WIDE, WIDE)
        copies.append(
            pltpu.make_async_copy(
                update.at[:, :, w], update_hbm.at[:, :, w], sems.at[4 + j]
            )
        )
        copies[-1].start()
    for copy in copies:
        copy.wait()


def body(grad_parts, left_basis, right_basis, first, second, left, right, table):
    hbm = pl.BlockSpec(memory_space=pltpu.HBM)
    vmem = pl.BlockSpec(memory_space=pltpu.VMEM)
    table_smem = pltpu.SMEM((2, N), I32)
    square = jax.ShapeDtypeStruct((B, B), F32)
    halves = [pltpu.VMEM((B, B), BF16)] * 12
    words, lines = pltpu.VMEM((N * 8, 128), I32), pltpu.VMEM((N, 1, 128), F32)
    dma = pltpu.SemaphoreType.DMA
    mids = pl.pallas_call(
        step_kernel,
        out_shape=(
            jax.ShapeDtypeStruct((N * 8, 128), I32),
            jax.ShapeDtypeStruct((N, 1, 128), F32),
            square, square, square, square,
        ),
        in_specs=[hbm] * 8,
        out_specs=(vmem,) * 6,
        scratch_shapes=[
            pltpu.VMEM((4, 16, 8192), BF16),
            *[pltpu.VMEM((B, B), F32)] * 6,
            table_smem,
            pltpu.VMEM((4, 8, 8192), F32),
            pltpu.VMEM((2, 16, 8192), BF16),
            pltpu.VMEM((2, 16, 8192), BF16),
            words, words, words,
            pltpu.VMEM((B, B), F32),
            *halves,
            words, lines,
            pltpu.SemaphoreType.REGULAR,
            dma((CHUNKS,)), dma((7,)), dma((CHUNKS,)), dma((CHUNKS,)),
            dma((1,)), dma((4, 1)), dma((2,)), dma((2,)),
        ],
        compiler_params=pltpu.CompilerParams(
            collective_id=0, has_side_effects=True, vmem_limit_bytes=49 * 2**20
        ),
    )(grad_parts, left_basis, right_basis, first, second, left, right, table)
    whole = jax.ShapeDtypeStruct((1, B, B), F32)
    return pl.pallas_call(
        write_kernel,
        out_shape=(
            jax.ShapeDtypeStruct((4, 8, 8192), F32), whole, whole, whole, whole
        ),
        in_specs=[vmem] * 6 + [hbm],
        out_specs=(hbm,) * 5,
        scratch_shapes=[
            words, pltpu.VMEM((N, 128), F32), pltpu.VMEM((4, 8, 8192), F32),
            table_smem, dma((9,)),
        ],
        compiler_params=pltpu.CompilerParams(vmem_limit_bytes=16 * 2**20),
    )(*mids, table)


def solution(mesh):
    owned = P(("replica", "fsdp"), None, None)
    return jax.shard_map(
        body,
        mesh=mesh,
        in_specs=(P("replica", "fsdp", None, None),) + (owned,) * 6 + (P(),),
        out_specs=(P("fsdp", "replica", None),) + (owned,) * 4,
        check_vma=False,
    )
```
